32 devices in a mesh: section: 2 (over core), dp: 16 (over z, y, x).
Axes of the slice: x: 2, y: 2, z: 4, core: 2. Of those that a mesh axis runs over, the one named last changes fastest.
Arguments:
- media: bfloat16 [128, 256, 1024], P('dp'), may hold values from -6 to 6
- image_live: int32 [128], P('dp'), may hold values 0 or 1
- start_latents: bfloat16 [64, 1024], replicated, may hold values from -6 to 6
- latent_cotangent: bfloat16 [128, 64, 1024], P('dp'), may hold values from -6 to 6
- media_gain: float32 [2, 1024], P('section'), may hold values from 0.5 to 1.5
- media_bias: float32 [2, 1024], P('section'), may hold values from -1.5 to 1.5
- latent_gain: float32 [2, 1024], P('section'), may hold values from 0.5 to 1.5
- latent_bias: float32 [2, 1024], P('section'), may hold values from -1.5 to 1.5
- w_query: bfloat16 [2, 1024, 512], P('section'), may hold values from -0.1875 to 0.1875
- w_kv: bfloat16 [2, 1024, 1024], P('section'), may hold values from -0.1875 to 0.1875
- w_out: bfloat16 [2, 512, 1024], P('section'), may hold values from -3 to 3
- ff_gain: float32 [2, 1024], P('section'), may hold values from 0.5 to 1.5
- ff_bias: float32 [2, 1024], P('section'), may hold values from -1.5 to 1.5
- w_up: bfloat16 [2, 1024, 4096], P('section'), may hold values from -0.1875 to 0.1875
- w_down: bfloat16 [2, 4096, 1024], P('section'), may hold values from -0.09375 to 0.09375
Outputs:
- layer_latents: bfloat16 [2, 128, 64, 1024], P('section', 'dp')
- media_grad: float32 [128, 256, 1024], P('dp', None, 'section')
- start_grad: float32 [64, 1024], P('section', 'dp')
- grad_media_gain: float32 [2, 1024], P('section', 'dp')
- grad_media_bias: float32 [2, 1024], P('section', 'dp')
- grad_latent_gain: float32 [2, 1024], P('section', 'dp')
- grad_latent_bias: float32 [2, 1024], P('section', 'dp')
- grad_query: float32 [2, 1024, 512], P('section', 'dp')
- grad_kv: float32 [2, 1024, 1024], P('section', 'dp')
- grad_out: float32 [2, 512, 1024], P('section', 'dp')
- grad_ff_gain: float32 [2, 1024], P('section', 'dp')
- grad_ff_bias: float32 [2, 1024], P('section', 'dp')
- grad_up: float32 [2, 1024, 4096], P('section', 'dp')
- grad_down: float32 [2, 4096, 1024], P('section', 'dp')
The draws below stay inside these ranges and needn't reach their ends.
All inputs are finite; a program needn't handle non-finite values. No bound on the sum of `image_live` on one device may be relied on, other than what follows from the above.
Results may differ from the reference program's by a relative error of at most 0.017.
Values may be sent and summed in bfloat16 or wider, within the bound.
A program may use at most 320 MiB of HBM per device.

```python
import jax
import jax.numpy as jnp
from jax import lax

D = 1024
FF = 4096
HEADS = 8
HEAD_DIM = 64
LATENTS = 64
P_SIZE = 256
INNER = 512
IMG_DEV = 8
IMAGES = 128


def place_ends(drawn, own_key, smallest, top_value):
    index_at = [jax.random.randint(jax.random.fold_in(own_key, axis), (), 0, length) for axis, length in enumerate(drawn.shape)]
    main_axis = drawn.shape.index(max(drawn.shape))
    neighbour = index_at[:main_axis] + [(index_at[main_axis] + 1) % drawn.shape[main_axis]] + index_at[main_axis + 1:]
    return drawn.at[tuple(index_at)].set(smallest).at[tuple(neighbour)].set(top_value)


def block_scale(stream_key, shape, shards, low, top_value):
    def one(dim, parts):
        heights = jax.random.uniform(jax.random.fold_in(jax.random.fold_in(stream_key, 6), dim), (parts,), jnp.float32, low / len(shards), top_value / len(shards))
        return jnp.repeat(jnp.exp(heights), shape[dim] // parts).reshape((-1,) + (1,) * (len(shape) - dim - 1))

    loudness = one(*shards[0])
    for cut in shards[1:]:
        loudness = loudness * one(*cut)
    return loudness


def bell_draw(rng, shape, scale, most, pieces=(), held_as=jnp.bfloat16):
    factor_of = block_scale(rng, shape, pieces, -0.22, 0.18) if pieces else 1.0
    drawn = jax.random.normal(rng, shape, jnp.float32) * scale * factor_of
    return jnp.minimum(jnp.maximum(drawn, -most), most).astype(held_as)


def setup_inputs(seed: int = 0) -> dict:
    splits = jax.random.split(jax.random.key(seed), 16)
    return {
        "media": bell_draw(splits[0], (IMAGES, P_SIZE, D), 1.0, 6.0, ((0, 16),)),
        "image_live": place_ends((jax.random.randint(splits[1], (IMAGES,), 0, 4) < 3).astype(jnp.int32), jax.random.fold_in(splits[1], 1), 0, 1),
        "start_latents": bell_draw(splits[2], (LATENTS, D), 1.0, 6.0),
        "latent_cotangent": bell_draw(splits[3], (IMAGES, LATENTS, D), 1.0, 6.0, ((0, 16),)),
        "media_gain": jnp.clip(1.0 + 0.1 * jax.random.normal(splits[4], (2, D), jnp.float32), 0.5, 1.5),
        "media_bias": bell_draw(splits[5], (2, D), 0.3, 1.5, ((0, 2),), jnp.float32),
        "latent_gain": jnp.clip(1.0 + 0.1 * jax.random.normal(splits[6], (2, D), jnp.float32), 0.5, 1.5),
        "latent_bias": bell_draw(splits[7], (2, D), 0.3, 1.5, ((0, 2),), jnp.float32),
        "w_query": bell_draw(splits[8], (2, D, INNER), D ** -0.5, 0.1875, ((0, 2),)),
        "w_kv": bell_draw(splits[9], (2, D, 2 * INNER), D ** -0.5, 0.1875, ((0, 2),)),
        "w_out": bell_draw(splits[10], (2, INNER, D), (max(INNER // 128, 2)) ** -0.5, 3.0, ((0, 2),)),
        "ff_gain": jnp.clip(1.0 + 0.1 * jax.random.normal(splits[11], (2, D), jnp.float32), 0.5, 1.5),
        "ff_bias": bell_draw(splits[12], (2, D), 0.3, 1.5, ((0, 2),), jnp.float32),
        "w_up": bell_draw(splits[13], (2, D, FF), D ** -0.5, 0.1875, ((0, 2),)),
        "w_down": bell_draw(splits[14], (2, FF, D), FF ** -0.5, 0.09375, ((0, 2),)),
    }


@jax.custom_vjp
def low(v):
    return lax.optimization_barrier(v.astype(jnp.bfloat16)).astype(jnp.float32)

@jax.custom_vjp
def low_back(v):
    return v

def low_keep(v):
    return (low(v), None)

def low_pass(kept, grad):
    return (grad,)

def back_keep(v):
    return (v, None)

def back_low(kept, grad):
    return (low(grad),)
low.defvjp(low_keep, low_pass)
low_back.defvjp(back_keep, back_low)

def round_both(value):
    return low(low_back(value))

def product(form, left, right):
    return jnp.einsum(form, left, right, precision=lax.Precision.HIGHEST)

def layer_norm(value, gain, offset):
    centred = value - lax.optimization_barrier(jnp.mean(value, axis=-1, keepdims=True))
    factor = lax.rsqrt(lax.optimization_barrier(jnp.mean(centred * centred, axis=-1, keepdims=True)) + 1e-05)
    return centred * factor * gain + offset

def resampler_layer(latent, media_rows, params):
    media_gain, media_bias, latent_gain, latent_bias, w_query, w_kv, w_out, ff_gain, ff_bias, w_up, w_down = params
    images = media_rows.shape[0]
    latent_rows = latent.shape[1]
    inner_width = w_query.shape[1]
    norm_media = low(layer_norm(media_rows, media_gain, media_bias))
    norm_latent = low(layer_norm(latent, latent_gain, latent_bias))
    query = round_both(product('bld,de->ble', norm_latent, w_query) * HEAD_DIM ** (-0.5))
    joined = jnp.concatenate([norm_media, norm_latent], axis=1)
    keyval = round_both(product('bnd,de->bne', joined, w_kv))
    query_heads = query.reshape(images, latent_rows, HEADS, HEAD_DIM)
    key_heads = keyval[..., :inner_width].reshape(images, -1, HEADS, HEAD_DIM)
    value_heads = keyval[..., inner_width:].reshape(images, -1, HEADS, HEAD_DIM)
    scores = low_back(product('blhe,bnhe->bhln', query_heads, key_heads))
    attn_prob = low(jax.nn.softmax(scores, axis=-1))
    attended = round_both(product('bhln,bnhe->blhe', attn_prob, value_heads).reshape(images, latent_rows, inner_width))
    mixed = latent + low_back(product('ble,ed->bld', attended, w_out))
    norm_ff = low(layer_norm(mixed, ff_gain, ff_bias))
    pre_act = low_back(product('bld,df->blf', norm_ff, w_up))
    hidden = low(jax.nn.gelu(pre_act, approximate=False))
    return mixed + low_back(product('blf,fd->bld', hidden, w_down))

def reference(media, image_live, start_latents, latent_cotangent, media_gain, media_bias, latent_gain, latent_bias, w_query, w_kv, w_out, ff_gain, ff_bias, w_up, w_down):
    stacked = tuple((entry.astype(jnp.float32) for entry in (media_gain, media_bias, latent_gain, latent_bias, w_query, w_kv, w_out, ff_gain, ff_bias, w_up, w_down)))

    def forward_all(start, media_all, *layer_params):
        first_params = tuple((entry[0] for entry in layer_params))
        second_params = tuple((entry[1] for entry in layer_params))

        def group_pass(media_group):
            begin = jnp.broadcast_to(start, (media_group.shape[0],) + start.shape)
            middle = round_both(resampler_layer(begin, media_group, first_params))
            return (resampler_layer(middle, media_group, second_params), middle)
        groups = media_all.reshape(IMAGES // IMG_DEV, IMG_DEV, P_SIZE, D)
        final, middle = lax.map(jax.checkpoint(group_pass), groups)
        return (final.reshape(IMAGES, LATENTS, D), middle.reshape(IMAGES, LATENTS, D))
    final, pullback, middle = jax.vjp(forward_all, start_latents.astype(jnp.float32), media.astype(jnp.float32), *stacked, has_aux=True)
    weighting = image_live.astype(jnp.float32)[:, None, None]
    grads = pullback(latent_cotangent.astype(jnp.float32) * weighting)
    layer_latents = jnp.stack([middle, final]).astype(jnp.bfloat16)
    return (layer_latents, grads[1], grads[0], grads[2], grads[3], grads[4], grads[5], grads[6], grads[7], grads[8], grads[9], grads[10], grads[11], grads[12])
```

```python
import functools

import jax
import jax.numpy as jnp
from jax import lax
from jax.experimental import pallas as pl
from jax.experimental.pallas import tpu as pltpu
from jax.sharding import PartitionSpec as P

MESH = pl.DeviceIdType.MESH
F32 = jnp.float32
BF16 = jnp.bfloat16
HEAD_DIM = 64
LANES = 256
GROUP = 4


def dot(left, right):
    return jnp.dot(left, right, preferred_element_type=F32)


def dot_rows(left, right):
    return lax.dot_general(left, right, (((1,), (1,)), ((), ())), preferred_element_type=F32)


def dot_cols(left, right):
    return lax.dot_general(left, right, (((0,), (0,)), ((), ())), preferred_element_type=F32)


def normed(value):
    centred = value - jnp.mean(value, axis=-1, keepdims=True)
    factor = lax.rsqrt(jnp.mean(centred * centred, axis=-1, keepdims=True) + 1e-05)
    return centred * factor, factor


def norm_back(upstream, hat, factor, gain):
    scaled = upstream * gain
    return factor * (
        scaled
        - jnp.mean(scaled, axis=-1, keepdims=True)
        - hat * jnp.mean(scaled * hat, axis=-1, keepdims=True)
    )


def gelu_and_slope(u):
    e = jnp.exp(-0.5 * (u * u))
    d = 1.0 + jnp.abs(u) * (0.3275911 * 0.7071067811865476)
    t = pl.reciprocal(d, approx=True)
    t = t * (2.0 - d * t)
    tail = t * (
        0.127414796 + t * (-0.142248368 + t * (0.7107068705 + t * (-0.7265760135 + t * 0.5307027145)))
    )
    tail = tail * e
    phi = jnp.where(u >= 0.0, 1.0 - tail, tail)
    return u * phi, phi + (u * e) * 0.3989422804014327


def layer_kernel(
    dims,
    start,
    media,
    g_in,
    vectors,
    wq,
    wkv,
    wo,
    wu,
    wd,
    y_out,
    j_out,
    o_out,
    f_out,
    h_out,
    du_out,
    dz1_out,
    dq_out,
    dkv_out,
    g_out,
    sums,
    start_sum,
    wq_v,
    wkv_v,
    wo_v,
    wu_v,
    wd_v,
    j_v,
    kv_v,
    z_v,
    q_v,
    p_v,
    o_v,
    z1_v,
    f_v,
    h_v,
    sl_v,
    y_v,
    acc,
    g_v,
    dz1_v,
    dq_v,
    do_v,
    dz_v,
    mask_v,
    load_sem,
    store_sem,
    send_sem,
    recv_sem,
):
    images, latents, patches, inner, hidden, step = dims
    rows = images * latents
    per = GROUP * latents
    batches = images // GROUP
    groups = inner // LANES
    heads = LANES // HEAD_DIM
    chunks = hidden // step
    section = lax.axis_index("section")
    dp = lax.axis_index("dp")
    sibling = (1 - section, dp)

    def load(k, src, dst):
        return pltpu.make_async_copy(src, dst, load_sem.at[k])

    loads = [
        load(0, wkv, wkv_v),
        load(1, wq, wq_v),
        load(2, wo, wo_v),
        load(3, wu, wu_v),
        load(4, wd, wd_v),
    ]

    def media_load(i):
        return load(6 + i, media.at[i], j_v.at[i, pl.ds(0, patches)])

    media_load(0).start()
    loads[0].start()
    for i in range(1, images):
        media_load(i).start()
    for copy in loads[1:]:
        copy.start()
    g_load = load(5, g_in, g_v)

    def start_load(i):
        return load(6 + images + i, start, z_v.at[pl.ds(i * latents, latents)])

    @pl.when(section == 0)
    def _():
        for i in range(images):
            start_load(i).start()

    @pl.when(section == 1)
    def _():
        g_load.start()

    barrier = pltpu.get_barrier_semaphore()
    pl.semaphore_signal(barrier, inc=1, device_id=sibling, device_id_type=MESH)

    row_head = lax.broadcasted_iota(jnp.int32, (heads * latents, LANES), 0) // latents
    lane_head = lax.broadcasted_iota(jnp.int32, (heads * latents, LANES), 1) // HEAD_DIM
    mask_v[...] = jnp.where(row_head == lane_head, 1.0, 0.0).astype(F32)
    sums[...] = jnp.zeros_like(sums)
    start_sum[...] = jnp.zeros_like(start_sum)

    loads[0].wait()

    def media_step(i, carry):
        media_load(i).wait()
        hat, _ = normed(j_v[i, pl.ds(0, patches), :].astype(F32))
        low = (hat * vectors[0:1, :] + vectors[1:2, :]).astype(BF16)
        j_v[i, pl.ds(0, patches), :] = low
        kv_v[i, pl.ds(0, patches), :] = dot(low, wkv_v[...]).astype(BF16)
        return carry

    lax.fori_loop(0, images, media_step, 0)
    for copy in loads[1:]:
        copy.wait()

    @pl.when(section == 0)
    def _():
        for i in range(images):
            start_load(i).wait()

    @pl.when(section == 1)
    def _():
        g_load.wait()

    pl.semaphore_wait(barrier, 1)

    def relay_latents(b):
        span = pl.ds(b * per, per)
        return pltpu.make_async_remote_copy(
            src_ref=y_v.at[span],
            dst_ref=z_v.at[span],
            send_sem=send_sem.at[b],
            recv_sem=recv_sem.at[b],
            device_id=sibling,
            device_id_type=MESH,
        )

    def relay_grad(b):
        span = pl.ds(b * per, per)
        return pltpu.make_async_remote_copy(
            src_ref=dz_v.at[span],
            dst_ref=g_v.at[span],
            send_sem=send_sem.at[batches + b],
            recv_sem=recv_sem.at[batches + b],
            device_id=sibling,
            device_id_type=MESH,
        )

    def spread(block):
        return (jnp.concatenate([block] * heads, axis=0).astype(F32) * mask_v[...]).astype(BF16)

    def gathered(block):
        kept = block * mask_v[...]
        total = kept[0:latents]
        for k in range(1, heads):
            total = total + kept[k * latents : (k + 1) * latents]
        return total

    def forward(b, carry):
        first = pl.multiple_of(b * per, per)
        span = pl.ds(first, per)

        @pl.when(section == 1)
        def _():
            relay_latents(b).wait_recv()

        z = z_v[span, :].astype(F32)
        hat, _ = normed(z)
        low = (hat * vectors[2:3, :] + vectors[3:4, :]).astype(BF16)
        j_v[pl.ds(b * GROUP, GROUP), pl.ds(patches, latents), :] = low.reshape(GROUP, latents, -1)
        q_v[span, :] = (dot(low, wq_v[...]) * HEAD_DIM**-0.5).astype(BF16)
        kv_v[pl.ds(b * GROUP, GROUP), pl.ds(patches, latents), :] = (
            dot(low, wkv_v[...]).astype(BF16).reshape(GROUP, latents, -1)
        )

        def attend(k, inner_carry):
            i = b * GROUP + k
            mine = pl.ds(pl.multiple_of(i * latents, latents), latents)
            for g in range(groups):
                lanes = slice(g * LANES, (g + 1) * LANES)
                values = slice(inner + g * LANES, inner + (g + 1) * LANES)
                scores = dot_rows(spread(q_v[mine, lanes]), kv_v[i, :, lanes])
                e = jnp.exp(scores - jnp.max(scores, axis=-1, keepdims=True))
                prob = (e / jnp.sum(e, axis=-1, keepdims=True)).astype(BF16)
                p_v[i * groups + g] = prob
                o_v[mine, lanes] = gathered(dot(prob, kv_v[i, :, values])).astype(BF16)
            return inner_carry

        lax.fori_loop(0, GROUP, attend, 0)
        mixed = z + dot(o_v[span, :], wo_v[...])
        z1_v[span, :] = mixed
        hat, _ = normed(mixed)
        low = (hat * vectors[4:5, :] + vectors[5:6, :]).astype(BF16)
        f_v[span, :] = low
        u = dot(low, wu_v[:, 0:step])
        for c in range(chunks):
            lanes = slice(c * step, (c + 1) * step)
            if c + 1 < chunks:
                later = dot(low, wu_v[:, (c + 1) * step : (c + 2) * step])
            h, slope = gelu_and_slope(u)
            h = h.astype(BF16)
            h_v[span, lanes] = h
            sl_v[span, lanes] = slope.astype(BF16)
            part = dot(h, wd_v[lanes, :])
            acc[...] = part + (mixed if c == 0 else acc[...])
            u = later
        y_v[span, :] = acc[...].astype(BF16)

        @pl.when(section == 0)
        def _():
            relay_latents(b).start()

        return carry

    lax.fori_loop(0, batches, forward, 0)

    def store(k, src, dst):
        return pltpu.make_async_copy(src, dst, store_sem.at[k])

    stores = [
        store(0, y_v, y_out),
        store(1, j_v, j_out),
        store(2, o_v, o_out),
        store(3, f_v, f_out),
        store(4, h_v, h_out),
    ]
    for copy in stores:
        copy.start()

    def backward(b, carry):
        first = pl.multiple_of(b * per, per)
        span = pl.ds(first, per)

        @pl.when(section == 0)
        def _():
            relay_grad(b).wait_recv()

        g = g_v[span, :]
        dh = dot_rows(g, wd_v[0:step, :])
        for c in range(chunks):
            lanes = slice(c * step, (c + 1) * step)
            if c + 1 < chunks:
                later = dot_rows(g, wd_v[(c + 1) * step : (c + 2) * step, :])
            du = (dh * sl_v[span, lanes].astype(F32)).astype(BF16)
            sl_v[span, lanes] = du
            part = dot_rows(du, wu_v[:, lanes])
            acc[...] = part if c == 0 else acc[...] + part
            dh = later
        df = acc[...]
        hat, factor = normed(z1_v[span, :])
        sums[4:5, :] += jnp.sum(df * hat, axis=0, keepdims=True)
        sums[5:6, :] += jnp.sum(df, axis=0, keepdims=True)
        dz1 = g.astype(F32) + norm_back(df, hat, factor, vectors[4:5, :])
        z1_v[span, :] = dz1
        low = dz1.astype(BF16)
        dz1_v[span, :] = low
        do_v[...] = dot_rows(low, wo_v[...]).astype(BF16)

        def attend(k, inner_carry):
            i = b * GROUP + k
            mine = pl.ds(pl.multiple_of(i * latents, latents), latents)
            local = pl.ds(pl.multiple_of(k * latents, latents), latents)
            for n in range(groups):
                lanes = slice(n * LANES, (n + 1) * LANES)
                values = slice(inner + n * LANES, inner + (n + 1) * LANES)
                prob = p_v[i * groups + n]
                wide = spread(do_v[local, lanes])
                keys = kv_v[i, :, lanes]
                dv = dot_cols(prob, wide)
                dp_ = dot_rows(wide, kv_v[i, :, values])
                pf = prob.astype(F32)
                ds = (pf * (dp_ - jnp.sum(pf * dp_, axis=-1, keepdims=True))).astype(BF16)
                dk = dot_cols(ds, spread(q_v[mine, lanes]))
                dq = gathered(dot(ds, keys)).astype(BF16)
                dq_v[mine, lanes] = dq * BF16(HEAD_DIM**-0.5)
                kv_v[i, :, lanes] = dk.astype(BF16)
                kv_v[i, :, values] = dv.astype(BF16)
            return inner_carry

        lax.fori_loop(0, GROUP, attend, 0)
        tail = kv_v[pl.ds(b * GROUP, GROUP), pl.ds(patches, latents), :].reshape(per, -1)
        dn = dot_rows(dq_v[span, :], wq_v[...]) + dot_rows(tail, wkv_v[...])
        hat, factor = normed(z_v[span, :].astype(F32))
        sums[2:3, :] += jnp.sum(dn * hat, axis=0, keepdims=True)
        sums[3:4, :] += jnp.sum(dn, axis=0, keepdims=True)
        dz = z1_v[span, :] + norm_back(dn, hat, factor, vectors[2:3, :])
        dz_v[span, :] = dz.astype(BF16)

        @pl.when(section == 1)
        def _():
            relay_grad(b).start()

        @pl.when(section == 0)
        def _():
            total = dz[0:latents]
            for k in range(1, GROUP):
                total = total + dz[k * latents : (k + 1) * latents]
            start_sum[...] += total

        return carry

    lax.fori_loop(0, batches, backward, 0)
    late = [
        store(5, sl_v, du_out),
        store(6, dz1_v, dz1_out),
        store(7, dq_v, dq_out),
        store(8, kv_v, dkv_out),
        store(9, g_v, g_out),
    ]
    for copy in late:
        copy.start()
    for copy in stores + late:
        copy.wait()

    @pl.when(section == 0)
    def _():
        for b in range(batches):
            relay_latents(b).wait_send()

    @pl.when(section == 1)
    def _():
        for b in range(batches):
            relay_grad(b).wait_send()


def layers(start, media, g_in, vectors, wq, wkv, wo, wu, wd, collective_id=2):
    images, patches, width = media.shape
    latents = start.shape[0]
    inner = wq.shape[1]
    hidden = wu.shape[1]
    rows = images * latents
    per = GROUP * latents
    batches = images // GROUP
    groups = inner // LANES
    step = 512
    dims = (images, latents, patches, inner, hidden, step)
    any_spec = pl.BlockSpec(memory_space=pl.ANY)
    vmem_spec = pl.BlockSpec(memory_space=pltpu.VMEM)
    keys = patches + latents

    def low(*shape):
        return jax.ShapeDtypeStruct(shape, BF16)

    out_shape = [
        low(rows, width),
        low(images, keys, width),
        low(rows, inner),
        low(rows, width),
        low(rows, hidden),
        low(rows, hidden),
        low(rows, width),
        low(rows, inner),
        low(images, keys, 2 * inner),
        low(rows, width),
        jax.ShapeDtypeStruct((8, width), F32),
        jax.ShapeDtypeStruct((latents, width), F32),
    ]
    scratch = [
        pltpu.VMEM(wq.shape, BF16),
        pltpu.VMEM(wkv.shape, BF16),
        pltpu.VMEM(wo.shape, BF16),
        pltpu.VMEM(wu.shape, BF16),
        pltpu.VMEM(wd.shape, BF16),
        pltpu.VMEM((images, keys, width), BF16),
        pltpu.VMEM((images, keys, 2 * inner), BF16),
        pltpu.VMEM((rows, width), BF16),
        pltpu.VMEM((rows, inner), BF16),
        pltpu.VMEM((images * groups, LANES // HEAD_DIM * latents, keys), BF16),
        pltpu.VMEM((rows, inner), BF16),
        pltpu.VMEM((rows, width), F32),
        pltpu.VMEM((rows, width), BF16),
        pltpu.VMEM((rows, hidden), BF16),
        pltpu.VMEM((rows, hidden), BF16),
        pltpu.VMEM((rows, width), BF16),
        pltpu.VMEM((per, width), F32),
        pltpu.VMEM((rows, width), BF16),
        pltpu.VMEM((rows, width), BF16),
        pltpu.VMEM((rows, inner), BF16),
        pltpu.VMEM((per, inner), BF16),
        pltpu.VMEM((rows, width), BF16),
        pltpu.VMEM((LANES // HEAD_DIM * latents, LANES), F32),
        pltpu.SemaphoreType.DMA((6 + 2 * images,)),
        pltpu.SemaphoreType.DMA((10,)),
        pltpu.SemaphoreType.DMA((2 * batches,)),
        pltpu.SemaphoreType.DMA((2 * batches,)),
    ]
    return pl.pallas_call(
        functools.partial(layer_kernel, dims),
        out_shape=out_shape,
        in_specs=[any_spec] * 3 + [vmem_spec] + [any_spec] * 5,
        out_specs=[any_spec] * 10 + [vmem_spec] * 2,
        scratch_shapes=scratch,
        compiler_params=pltpu.CompilerParams(
            collective_id=collective_id, has_side_effects=True, vmem_limit_bytes=62 * 1024 * 1024
        ),
        name="layers",
    )(start, media, g_in, vectors, wq, wkv, wo, wu, wd)


def rs_kernel(specs, width, *refs):
    count = len(specs)
    sources = refs[:width]
    outs = refs[width : 2 * width]
    scratch = refs[2 * width :]
    buffers = [scratch[5 * i : 5 * i + 5] for i in range(count)]
    load_sem, send_sem, recv_sem = scratch[5 * count :]
    section = lax.axis_index("section")
    dp = lax.axis_index("dp")
    x = lax.rem(dp, 2)
    y = lax.rem(dp // 2, 2)
    z = dp // 4
    at_x = (section, dp + 1 - 2 * x)
    at_y = (section, dp + 2 - 4 * y)
    at_up = (section, dp + 4)
    at_down = (section, dp - 4)

    barrier = pltpu.get_barrier_semaphore()
    pl.semaphore_signal(barrier, inc=1, device_id=at_x, device_id_type=MESH)
    pl.semaphore_signal(barrier, inc=1, device_id=at_y, device_id_type=MESH)

    @pl.when(z < 3)
    def _():
        pl.semaphore_signal(barrier, inc=1, device_id=at_up, device_id_type=MESH)

    @pl.when(z > 0)
    def _():
        pl.semaphore_signal(barrier, inc=1, device_id=at_down, device_id_type=MESH)

    pl.semaphore_wait(barrier, 2 + jnp.where(z < 3, 1, 0) + jnp.where(z > 0, 1, 0))

    def remote(i, slot, src, dst, where):
        return pltpu.make_async_remote_copy(
            src_ref=src,
            dst_ref=dst,
            send_sem=send_sem.at[i, slot],
            recv_sem=recv_sem.at[i, slot],
            device_id=where,
            device_id_type=MESH,
        )

    def window(i):
        spec = specs[i]
        ref = sources[spec["array"]]
        (r0, rn), (c0, cn) = spec["rows"], spec["cols"]
        return ref.at[:, :, :, pl.ds(r0, rn), pl.ds(c0, cn)]

    def target(i):
        spec = specs[i]
        ref = outs[spec["array"]]
        (r0, rn), (c0, cn) = spec["rows"], spec["cols"]
        return ref.at[pl.ds(r0, rn), pl.ds(c0, cn)]

    def load(i):
        spec = specs[i]
        own = buffers[i][0]
        src = window(i)
        if spec["order"] == "xyz":
            part = src.at[:, :, x]
        elif spec["order"] == "yxz":
            part = src.at[:, y]
        else:
            part = src
        return pltpu.make_async_copy(part, own, load_sem.at[i])

    def first_copy(i):
        spec = specs[i]
        own, first, second, plus, minus = buffers[i]
        src = window(i)
        if spec["order"] == "xyz":
            return remote(i, 0, src.at[:, :, 1 - x], first, at_x)
        if spec["order"] == "yxz":
            return remote(i, 0, src.at[:, 1 - y], first, at_y)
        if spec["order"] == "zxy":
            return remote(i, 0, plus.at[z, :, 1 - x], first, at_x)
        return remote(i, 0, plus.at[z, 1 - y], first, at_y)

    def second_copy(i):
        spec = specs[i]
        own, first, second, plus, minus = buffers[i]
        if spec["order"] == "xyz":
            return remote(i, 1, first.at[:, 1 - y], second, at_y)
        if spec["order"] == "yxz":
            return remote(i, 1, first.at[:, 1 - x], second, at_x)
        if spec["order"] == "zxy":
            return remote(i, 1, first.at[1 - y], second, at_y)
        return remote(i, 1, first.at[1 - x], second, at_x)

    def add_any(dst, left, right):
        lead = dst.shape[:-2]
        total = 1
        for size in lead:
            total *= size

        def step(k, carry):
            at = []
            rest = k
            for size in reversed(lead):
                at.append(lax.rem(rest, size))
                rest = rest // size
            at = tuple(reversed(at))
            dst[at] = (left[at].astype(F32) + right[at].astype(F32)).astype(dst.dtype)
            return carry

        if total == 1:
            at = (0,) * len(lead)
            dst[at] = (left[at].astype(F32) + right[at].astype(F32)).astype(dst.dtype)
        else:
            lax.fori_loop(0, total, step, 0)

    def z_base(i):
        return buffers[i][0] if specs[i]["order"][0] == "z" else buffers[i][2]

    def up_copy(i, d, src):
        return remote(i, 2 + d, src, buffers[i][3].at[d], at_up)

    def down_copy(i, d, src):
        return remote(i, 6 + d, src, buffers[i][4].at[d], at_down)

    def z_start(i):
        base = z_base(i)

        @pl.when(z == 0)
        def _():
            for d in (3, 2, 1):
                up_copy(i, d, base.at[d]).start()

        @pl.when(z == 3)
        def _():
            for d in (0, 1, 2):
                down_copy(i, d, base.at[d]).start()

    def pass_up(i, d):
        base, plus = z_base(i), buffers[i][3]
        copy = up_copy(i, d, plus.at[d])
        copy.wait_recv()
        add_any(plus.at[d], plus.at[d], base.at[d])
        copy.start()

    def pass_down(i, d):
        base, minus = z_base(i), buffers[i][4]
        copy = down_copy(i, d, minus.at[d])
        copy.wait_recv()
        add_any(minus.at[d], minus.at[d], base.at[d])
        copy.start()

    def z_near(i):
        @pl.when(z == 1)
        def _():
            for d in (3, 2):
                pass_up(i, d)

        @pl.when(z == 2)
        def _():
            for d in (0, 1):
                pass_down(i, d)

    def z_far(i):
        @pl.when(z == 2)
        def _():
            pass_up(i, 3)

        @pl.when(z == 1)
        def _():
            pass_down(i, 0)

    def z_arrive(i):
        plus, minus = buffers[i][3], buffers[i][4]

        @pl.when(z > 0)
        def _():
            up_copy(i, z, plus.at[z]).wait_recv()

        @pl.when(z < 3)
        def _():
            down_copy(i, z, minus.at[z]).wait_recv()

    def z_sum(i, at, base):
        plus, minus = buffers[i][3], buffers[i][4]
        from_low = plus[(z,) + at].astype(F32)
        from_high = minus[(z,) + at].astype(F32)
        mine = base[(z,) + at].astype(F32)
        return mine + from_low + from_high

    def stage(i, step):
        spec = specs[i]
        own, first, second, plus, minus = buffers[i]
        order = spec["order"]
        if order[0] == "z":
            if step == 0:
                load(i).start()
            elif step == 1:
                load(i).wait()
                z_start(i)
            elif step == 2:
                z_near(i)
            elif step == 3:
                z_far(i)
            elif step == 4:
                z_arrive(i)
                for a in range(2):
                    for b in range(2):
                        plus[z, a, b] = z_sum(i, (a, b), own).astype(plus.dtype)
                first_copy(i).start()
            elif step == 5:
                first_copy(i).wait_recv()
                for a in range(2):
                    mine = plus[z, a, x] if order[1] == "x" else plus[z, y, a]
                    first[a] = (mine.astype(F32) + first[a].astype(F32)).astype(first.dtype)
                second_copy(i).start()
            elif step == 6:
                second_copy(i).wait_recv()
                mine = first[y] if order[1] == "x" else first[x]
                target(i)[...] = mine.astype(F32) + second[...].astype(F32)
        else:
            if step == 0:
                load(i).start()
                first_copy(i).start()
            elif step == 1:
                load(i).wait()
                first_copy(i).wait_recv()
                add_any(first, first, own)
                second_copy(i).start()
            elif step == 2:
                second_copy(i).wait_recv()
                mine = y if order == "xyz" else x

                def merge(k, carry):
                    second[k] = (second[k].astype(F32) + first[k, mine].astype(F32)).astype(
                        second.dtype
                    )
                    return carry

                lax.fori_loop(0, 4, merge, 0)
                z_start(i)
            elif step == 3:
                z_near(i)
            elif step == 4:
                z_far(i)
            elif step == 5:
                z_arrive(i)
                target(i)[...] = z_sum(i, (), second)

    @pl.when(z == 0)
    def _():
        for i in range(count):
            plus = buffers[i][3]
            plus[0] = jnp.zeros(plus.shape[1:], plus.dtype)

    @pl.when(z == 3)
    def _():
        for i in range(count):
            minus = buffers[i][4]
            minus[3] = jnp.zeros(minus.shape[1:], minus.dtype)

    last = max(spec["slot"] for spec in specs) + 7
    for slot in range(last):
        live = [(slot - spec["slot"], i) for i, spec in enumerate(specs)]
        live = [(step, i) for step, i in live if 0 <= step <= 6]
        for step, i in [e for e in live if e[0] == 0]:
            stage(i, step)
        for step, i in sorted([e for e in live if e[0] > 0], key=lambda e: (-e[0], e[1])):
            stage(i, step)

    for i in range(count):
        first_copy(i).wait_send()
        second_copy(i).wait_send()
        base = z_base(i)
        for d in (3, 2, 1):

            @pl.when(z < d)
            def _():
                up_copy(i, d, base.at[d]).wait_send()

        for d in (0, 1, 2):

            @pl.when(z > d)
            def _():
                down_copy(i, d, base.at[d]).wait_send()


def plan(shapes, chunks=8):
    (ur, uc), (dr, dc) = shapes[0], shapes[1]
    specs = []
    for k in range(chunks):
        wide, tall = uc // chunks, dr // chunks
        specs.append(dict(array=0, rows=(0, ur), cols=(k * wide, wide), order="xyz", slot=k))
        specs.append(dict(array=1, rows=(k * tall, tall), cols=(0, dc), order="yxz", slot=k))
    rest = [(2, 4), (3, 2), (4, 2)]
    slots = iter((0, 0, 1, 1, 2, 3, 4, 5))
    for array, parts in rest:
        height, wide = shapes[array][0], shapes[array][1] // parts
        for k in range(parts):
            order = "zxy" if k % 2 else "zyx"
            specs.append(
                dict(array=array, rows=(0, height), cols=(k * wide, wide), order=order, slot=next(slots))
            )
    height, wide = shapes[5]
    specs.append(dict(array=5, rows=(0, height), cols=(0, wide), order="xyz", slot=1))
    return specs


def reduce_scatter(arrays, collective_id=1):
    shapes = [a.shape[1:] for a in arrays]
    specs = plan(shapes)
    views = [a.reshape((4, 2, 2) + a.shape[1:]) for a in arrays]
    scratch = []
    for spec in specs:
        tile = (spec["rows"][1], spec["cols"][1])
        kind = arrays[spec["array"]].dtype
        if spec["order"][0] == "z":
            full = [(4, 2, 2), (2,), (), (4, 2, 2), (4, 2, 2)]
        else:
            full = [(4, 2), (4, 2), (4,), (4,), (4,)]
        scratch += [pltpu.VMEM(lead + tile, kind) for lead in full]
    count = len(specs)
    scratch += [
        pltpu.SemaphoreType.DMA((count,)),
        pltpu.SemaphoreType.DMA((count, 10)),
        pltpu.SemaphoreType.DMA((count, 10)),
    ]
    return pl.pallas_call(
        functools.partial(rs_kernel, specs, len(arrays)),
        out_shape=[jax.ShapeDtypeStruct(s, F32) for s in shapes],
        in_specs=[pl.BlockSpec(memory_space=pl.ANY)] * len(arrays),
        out_specs=[pl.BlockSpec(memory_space=pltpu.VMEM)] * len(arrays),
        scratch_shapes=scratch,
        compiler_params=pltpu.CompilerParams(
            collective_id=collective_id, has_side_effects=True, vmem_limit_bytes=60 * 1024 * 1024
        ),
        name="sum_shards",
    )(*views)


def media_kernel(dims, dkv, media, wkv, gain, mine, other, sums):
    patches, half = dims
    section = lax.axis_index("section")

    @pl.when(pl.program_id(0) == 0)
    def _():
        sums[...] = jnp.zeros_like(sums)

    dj = dot_rows(dkv[0], wkv[...])
    hat, factor = normed(media[0].astype(F32))
    sums[0:1, :] += jnp.sum(dj * hat, axis=0, keepdims=True)
    sums[1:2, :] += jnp.sum(dj, axis=0, keepdims=True)
    grad = norm_back(dj, hat, factor, gain[...])

    @pl.when(section == 0)
    def _():
        mine[0] = grad[:, :half]
        other[0] = grad[:, half:].astype(BF16)

    @pl.when(section == 1)
    def _():
        mine[0] = grad[:, half:]
        other[0] = grad[:, :half].astype(BF16)


def media_grads(dkv, media, wkv, gain):
    images, patches, width = media.shape
    half = width // 2
    return pl.pallas_call(
        functools.partial(media_kernel, (patches, half)),
        grid=(images,),
        out_shape=[
            jax.ShapeDtypeStruct((images, patches, half), F32),
            jax.ShapeDtypeStruct((images, patches, half), BF16),
            jax.ShapeDtypeStruct((8, width), F32),
        ],
        in_specs=[
            pl.BlockSpec((1, patches, dkv.shape[2]), lambda i: (i, 0, 0)),
            pl.BlockSpec((1, patches, width), lambda i: (i, 0, 0)),
            pl.BlockSpec(wkv.shape, lambda i: (0, 0)),
            pl.BlockSpec((1, width), lambda i: (0, 0)),
        ],
        out_specs=[
            pl.BlockSpec((1, patches, half), lambda i: (i, 0, 0)),
            pl.BlockSpec((1, patches, half), lambda i: (i, 0, 0)),
            pl.BlockSpec((8, width), lambda i: (0, 0)),
        ],
        compiler_params=pltpu.CompilerParams(vmem_limit_bytes=48 * 1024 * 1024),
        name="media_grads",
    )(dkv, media, wkv, gain)


def weight_grad(left, right):
    left = left.reshape(-1, left.shape[-1])
    right = right.reshape(-1, right.shape[-1])
    return dot_cols(left, right).astype(BF16)


def shards(
    media,
    image_live,
    start_latents,
    latent_cotangent,
    media_gain,
    media_bias,
    latent_gain,
    latent_bias,
    w_query,
    w_kv,
    w_out,
    ff_gain,
    ff_bias,
    w_up,
    w_down,
):
    images, patches, width = media.shape
    latents = start_latents.shape[0]
    peers = lax.axis_size("dp")
    rows = images * latents
    target = (latent_cotangent * image_live.astype(BF16)[:, None, None]).reshape(rows, width)
    blank = jnp.zeros((1, width), F32)
    vectors = jnp.concatenate(
        [media_gain, media_bias, latent_gain, latent_bias, ff_gain, ff_bias, blank, blank], axis=0
    )
    wq, wkv, wo, wu, wd = w_query[0], w_kv[0], w_out[0], w_up[0], w_down[0]
    y, j, o, f, h, du, dz1, dq, dkv, g, sums, start_sum = layers(
        start_latents, media, target, vectors, wq, wkv, wo, wu, wd
    )
    mine, other, media_sums = media_grads(dkv, media, wkv, media_gain)
    theirs = lax.ppermute(other, "section", [(0, 1), (1, 0)])
    grad_up = weight_grad(f, du)
    grad_down = weight_grad(h, g)
    grad_kv = weight_grad(j, dkv)
    grad_query = weight_grad(j[:, patches:], dq)
    grad_out = weight_grad(o, dz1)
    lines = jnp.concatenate([media_sums[:2], sums[2:6]], axis=0)
    if peers == 16:
        part = width // peers
        small = jnp.concatenate(
            [lines.reshape(6, peers, part).swapaxes(0, 1).reshape(peers, -1),
             start_sum.reshape(latents, peers, part).swapaxes(0, 1).reshape(peers, -1)],
            axis=1,
        )
        small = jnp.pad(small, ((0, 0), (0, 40 * 128 - small.shape[1]))).reshape(peers, 40, 128)

        def cut(a):
            return a.reshape((peers, a.shape[0] // peers) + a.shape[1:])

        up, down, kv, query, out, small = reduce_scatter(
            [cut(grad_up), cut(grad_down), cut(grad_kv), cut(grad_query), cut(grad_out), small]
        )
        small = small.reshape(-1)
        lines = small[: 6 * part].reshape(6, part)
        start_part = small[6 * part : (6 + latents) * part].reshape(latents, part)
    else:
        up, down, kv, query, out = (
            lax.psum_scatter(a, "dp", scatter_dimension=0, tiled=True).astype(F32)
            for a in (grad_up, grad_down, grad_kv, grad_query, grad_out)
        )
        lines = lax.psum_scatter(lines, "dp", scatter_dimension=1, tiled=True)
        start_part = lax.psum_scatter(start_sum, "dp", scatter_dimension=1, tiled=True)
    first = lax.axis_index("section") == 0
    half = latents // 2
    far = lax.ppermute(start_part[half:], "section", [(0, 1), (1, 0)])
    start_grad = jnp.where(first, start_part[:half], far)
    media_grad = mine + theirs.astype(F32)
    return (
        y.reshape(1, images, latents, width),
        media_grad,
        start_grad,
        lines[0:1],
        lines[1:2],
        lines[2:3],
        lines[3:4],
        query[None],
        kv[None],
        out[None],
        lines[4:5],
        lines[5:6],
        up[None],
        down[None],
    )


def solution(mesh):
    row = P("section", None)
    mat = P("section", None, None)
    in_specs = (
        P("dp", None, None), P("dp"), P(), P("dp", None, None),
        row, row, row, row, mat, mat, mat, row, row, mat, mat,
    )
    line = P("section", "dp")
    block = P("section", "dp", None)
    out_specs = (
        P("section", "dp", None, None), P("dp", None, "section"), line,
        line, line, line, line, block, block, block, line, line, block, block,
    )
    return jax.shard_map(shards, mesh=mesh, in_specs=in_specs, out_specs=out_specs, check_vma=False)
```

```python
import functools

import jax
import jax.numpy as jnp
from jax import lax
from jax.experimental import pallas as pl
from jax.experimental.pallas import tpu as pltpu
from jax.sharding import PartitionSpec as P

MESH = pl.DeviceIdType.MESH
F32 = jnp.float32
BF16 = jnp.bfloat16
HEAD_DIM = 64
LANES = 256
GROUP = 4
TOGETHER = 4
STEP = 512
VMEM_LIMIT = 63 * 1024 * 1024


def dot(left, right):
    return jnp.dot(left, right, preferred_element_type=F32)


def dot_rows(left, right):
    return lax.dot_general(left, right, (((1,), (1,)), ((), ())), preferred_element_type=F32)


def dot_cols(left, right):
    return lax.dot_general(left, right, (((0,), (0,)), ((), ())), preferred_element_type=F32)


def normed(value):
    centred = value - jnp.mean(value, axis=-1, keepdims=True)
    factor = lax.rsqrt(jnp.mean(centred * centred, axis=-1, keepdims=True) + 1e-05)
    return centred * factor, factor


def norm_back(upstream, hat, factor, gain):
    scaled = upstream * gain
    return factor * (
        scaled
        - jnp.mean(scaled, axis=-1, keepdims=True)
        - hat * jnp.mean(scaled * hat, axis=-1, keepdims=True)
    )


def gelu_and_slope(u):
    e = jnp.exp2((u * u) * (-0.5 * 1.4426950408889634))
    t = pl.reciprocal(1.0 + jnp.abs(u) * (0.3275911 * 0.7071067811865476), approx=True)
    tail = t * (
        0.127414796 + t * (-0.142248368 + t * (0.7107068705 + t * (-0.7265760135 + t * 0.5307027145)))
    )
    tail = tail * e
    phi = jnp.where(u >= 0.0, 1.0 - tail, tail)
    return u * phi, phi + (u * e) * 0.3989422804014327


def halves(a, b):
    return (a.astype(F32) + b.astype(F32)).astype(a.dtype)


class Refs:
    def __init__(self, names, refs):
        self.__dict__.update(zip(names, refs, strict=True))


UP, DOWN, ATT, SMALL = 0, 1, 2, 3
CHUNKS = 8
RING = 4
DOWN_Z = 6
DOWN_SLOTS = (0, 0, 1, 1, 2, 2, 5, 5)
UP_SLOTS = (2, 2, 3, 3, 4, 4, 5, 5)
ATT_SLOTS = (3, 3, 4, 4, 1, 1, 2, 2)
MEDIA_SLOTS = (0, 0, 1, 1, 2, 3, 4, 4)
SMALL_SLOT = 5
BLOCKS = [(kind, c) for kind in (UP, DOWN, ATT) for c in range(CHUNKS)] + [(SMALL, 0)]


def layer_kernel(dims, fused, names, *all_refs):
    images, latents, patches, inner, hidden, width = dims
    r = Refs(names, all_refs)
    rows = images * latents
    per = GROUP * latents
    batches = images // GROUP
    groups = inner // LANES
    heads = LANES // HEAD_DIM
    chunks = hidden // STEP
    section = lax.axis_index("section")
    dp = lax.axis_index("dp")
    sibling = (1 - section, dp)
    x = lax.rem(dp, 2)
    y = lax.rem(dp // 2, 2)
    z = dp // 4
    at_x = (section, dp + 1 - 2 * x)
    at_y = (section, dp + 2 - 4 * y)
    at_up = (section, dp + 4)
    at_down = (section, dp - 4)
    j_v, kv_v, o_v, f_v, h_v, sl_v = r.j_v, r.kv_v, r.o_v, r.f_v, r.h_v, r.sl_v
    g_v, dz1_v, dq_v, wkv_v = r.g_v, r.dz1_v, r.dq_v, r.wkv_v

    def signal(sem, where):
        pl.semaphore_signal(sem, inc=1, device_id=where, device_id_type=MESH)

    def load(k, src, dst):
        return pltpu.make_async_copy(src, dst, r.load_sem.at[k])

    def store(k, src, dst):
        return pltpu.make_async_copy(src, dst, r.store_sem.at[k])

    def media_load(i):
        return load(6 + i, r.media.at[i], j_v.at[i, pl.ds(0, patches)])

    barrier = pltpu.get_barrier_semaphore()

    def greet():
        signal(barrier, sibling)
        if fused:
            signal(barrier, at_x)
            signal(barrier, at_y)

            @pl.when(z < 3)
            def _():
                signal(barrier, at_up)

            @pl.when(z > 0)
            def _():
                signal(barrier, at_down)

    def met():
        peers = 1
        if fused:
            peers = 3 + jnp.where(z < 3, 1, 0) + jnp.where(z > 0, 1, 0)
        pl.semaphore_wait(barrier, peers)


    def remote(kind, c, slot, src, dst, where):
        sem = sem_of(kind, c)
        along = not isinstance(slot, int) or 2 <= slot < 7
        sent = 2 * len(BLOCKS) + kind if along else sem + (len(BLOCKS) if slot == 1 else 0)
        return pltpu.make_async_remote_copy(
            src_ref=src,
            dst_ref=dst,
            send_sem=r.rs_send.at[sent],
            recv_sem=r.rs_recv.at[sem, slot],
            device_id=where,
            device_id_type=MESH,
        )

    def sem_of(kind, c):
        return BLOCKS.index((kind, c))

    def base_of(kind, c):
        return r.base_a.at[c % RING] if kind == ATT else r.base_s

    def before(kind, c):
        return (c - RING) if ATT_SLOTS[0] < ATT_SLOTS[RING] or kind == UP else (c + RING)

    def order_of(kind, c):
        if kind == DOWN:
            return "zx" if c < DOWN_Z else "yxz"
        return "yxz" if kind == ATT and c >= 4 else "xyz"

    def first_of(kind, c):
        if kind == SMALL:
            return r.first_s
        return {UP: r.first_u.at[c % RING], DOWN: r.first_d.at[c], ATT: r.first_a.at[c]}[kind]

    def second_of(kind, c):
        if kind == DOWN:
            return r.second_d.at[c - DOWN_Z]
        return r.second_s if kind == SMALL else {UP: r.second_u, ATT: r.second_a}[kind].at[c]

    def z_of(kind, c):
        if kind == DOWN:
            return r.z_d.at[c] if c < DOWN_Z else r.z_d_late.at[c - DOWN_Z]
        return r.z_s if kind == SMALL else {UP: r.z_u, ATT: r.z_a}[kind].at[c]

    def paired(kind, c):
        return kind == UP or (kind == DOWN and c >= DOWN_Z)

    def compute(kind, c):
        both = [c, c + 1]
        if kind in (UP, DOWN):
            if kind == UP:
                part = dot_cols(f_v[...], sl_v[4 * x + c // 2])
                part = part + dot_cols(r.fn_v[...], r.un_v[c // 2])
            else:
                side, q = c // 4, c % 4
                tall = hidden // 32
                at = [
                    (k, slice((2 * i + side) * tall, (2 * i + side + 1) * tall))
                    for k in range(4)
                    for i in range(2)
                ]
                columns = slice(q * LANES, (q + 2) * LANES)
                own = jnp.concatenate([h_v[2 * k + y, :, lanes] for k, lanes in at], axis=1)
                theirs = jnp.concatenate([r.hn_v[k, :, lanes] for k, lanes in at], axis=1)
                part = dot_cols(own, g_v[:, columns]) + dot_cols(theirs, r.gn_v[:, columns])
            for n, k in enumerate(both):
                first = first_of(kind, k)
                block = part[:, n * LANES : (n + 1) * LANES].astype(BF16)
                first[...] = block.reshape(first.shape)
        elif kind == ATT and c == 2:
            part = dot_cols(o_v[...], dz1_v[...]).astype(BF16)
            tall = inner // 16
            for n in range(4):
                base = base_of(kind, c + n // 2)
                block = part[:, n * LANES : (n + 1) * LANES]
                n = n % 2
                base[:, :, :, n * tall : (n + 1) * tall, :] = block.reshape(
                    base.shape[:3] + (tall, LANES)
                )
        elif kind == ATT:
            if c == 0:
                left = j_v[:, pl.ds(patches, latents), :].reshape(rows, width)
                part = dot_cols(left, dq_v[...])
            else:
                keys = images * (patches + latents)
                at = (c - 4) * LANES
                right = kv_v[:, :, at : at + 2 * LANES].reshape(keys, 2 * LANES)
                part = dot_cols(j_v[...].reshape(keys, width), right)
            for n, k in enumerate(both):
                base = base_of(kind, k)
                block = part[:, n * LANES : (n + 1) * LANES].astype(BF16)
                base[...] = block.reshape(base.shape)
        else:
            lines = r.lines[...]
            for j in range(16):
                own = lines[:, j * 64 : (j + 1) * 64]
                value = jnp.concatenate([own[:40], own[40:]], axis=1)
                r.base_s[j // 4, j // 2 % 2, j % 2] = value

    def first_copy(kind, c):
        base, first = base_of(kind, c), first_of(kind, c)
        if order_of(kind, c) == "xyz":
            return remote(kind, c, 0, base.at[:, :, 1 - x], first, at_x)
        return remote(kind, c, 0, base.at[:, 1 - y], first, at_y)

    def second_copy(kind, c):
        first, second = first_of(kind, c), second_of(kind, c)
        if order_of(kind, c) == "xyz":
            return remote(kind, c, 1, first.at[:, 1 - y], second, at_y)
        return remote(kind, c, 1, first.at[:, 1 - x], second, at_x)

    def end_copy(kind, c):
        if kind == UP:
            return remote(UP, c, 7, r.end_src.at[c], r.end_u.at[c], at_x)
        return remote(DOWN, c, 7, r.z_d.at[c, z, 1 - x], r.end_d.at[c], at_x)

    def begin(kind, c):
        both = [c] if kind == SMALL else [c, c + 1]
        for k in both:
            old = before(kind, k)
            if kind == UP and 0 <= old < CHUNKS:
                second_copy(UP, old).wait_send()
            if kind == ATT and 0 <= old < CHUNKS:
                first_copy(ATT, old).wait_send()
        compute(kind, c)
        for k in both:
            if paired(kind, k):
                second_copy(kind, k).start()
            elif kind == DOWN:
                z_start(kind, k)
            else:
                first_copy(kind, k).start()

    def exchange(k, b, src, dst, where):
        return pltpu.make_async_remote_copy(
            src_ref=src,
            dst_ref=dst,
            send_sem=r.pair_send.at[k, b],
            recv_sem=r.pair_recv.at[k, b],
            device_id=where,
            device_id_type=MESH,
        )

    def span_of(b):
        return pl.ds(pl.multiple_of(b * per, per), per)

    def exchange_f(b):
        return exchange(0, b, f_v.at[span_of(b)], r.fn_v.at[span_of(b)], at_x)

    def exchange_u(b):
        src = sl_v.at[pl.ds(4 * (1 - x), 4), span_of(b)]
        return exchange(1, b, src, r.un_v.at[:, span_of(b)], at_x)

    def exchange_g(b):
        return exchange(2, b, g_v.at[span_of(b)], r.gn_v.at[span_of(b)], at_y)

    def exchange_h(b):
        src = h_v.reshape(4, 2, rows, STEP).at[:, 1 - y, span_of(b)]
        return exchange(3, b, src, r.hn_v.at[:, span_of(b)], at_y)


    def phase_one(wq_v, wo_v, wu_v, wd_v, z_v, q_v, p_v, z1_v, y_v, acc, do_v, mask_v):
        greet()
        loads = [
            load(0, r.wkv, wkv_v),
            load(1, r.wq, wq_v),
            load(2, r.wo, wo_v),
            load(3, r.wu, wu_v),
            load(4, r.wd, wd_v),
        ]
        media_load(0).start()
        loads[0].start()
        for i in range(1, images):
            media_load(i).start()
        for copy in loads[1:]:
            copy.start()
        g_load = load(5, r.cotangent, g_v)

        def start_load(i):
            return load(6 + images, r.start, z_v.at[pl.ds(i * latents, latents)])

        @pl.when(section == 0)
        def _():
            for i in range(images):
                start_load(i).start()

        @pl.when(section == 1)
        def _():
            g_load.start()

        row_head = lax.broadcasted_iota(jnp.int32, (heads * latents, LANES), 0) // latents
        lane_head = lax.broadcasted_iota(jnp.int32, (heads * latents, LANES), 1) // HEAD_DIM
        mask_v[...] = jnp.where(row_head == lane_head, 1.0, 0.0).astype(BF16)
        r.lines[...] = jnp.zeros_like(r.lines)

        loads[0].wait()

        pieces = 4
        tall = patches // pieces
        wide = 2 * inner // pieces

        def media_piece(i, n):
            span = slice(n * tall, (n + 1) * tall)
            hat, _ = normed(j_v[i, span, :].astype(F32))
            low = (hat * r.media_gain[...] + r.media_bias[...]).astype(BF16)
            j_v[i, span, :] = low
            return low

        def media_all():
            media_load(0).wait()
            low = jnp.concatenate([media_piece(0, n) for n in range(pieces)], axis=0)
            for i in range(images):
                later = []
                if i + 1 < images:
                    media_load(i + 1).wait()
                for n in range(pieces):
                    lanes = slice(n * wide, (n + 1) * wide)
                    kv_v[i, :patches, lanes] = dot(low, wkv_v[:, lanes]).astype(BF16)
                    if i + 1 < images:
                        later.append(media_piece(i + 1, n))
                if later:
                    low = jnp.concatenate(later, axis=0)

        media_all()
        for copy in loads[1:]:
            copy.wait()

        @pl.when(section == 0)
        def _():
            load(6 + images, z_v, z_v).wait()

        @pl.when(section == 1)
        def _():
            g_load.wait()
            for i in range(images):
                span = slice(i * latents, (i + 1) * latents)
                live = r.live[i].astype(F32)
                g_v[span, :] = (g_v[span, :].astype(F32) * live).astype(BF16)

        met()
        if fused:

            @pl.when(section == 1)
            def _():
                for b in range(batches):
                    exchange_g(b).start()


        def relay_latents(b):
            span = pl.ds(b * per, per)
            return pltpu.make_async_remote_copy(
                src_ref=y_v.at[span],
                dst_ref=z_v.at[span],
                send_sem=r.send_sem.at[b],
                recv_sem=r.recv_sem.at[b],
                device_id=sibling,
                device_id_type=MESH,
            )

        def relay_grad(b):
            span = pl.ds(b * per, per)
            return pltpu.make_async_remote_copy(
                src_ref=y_v.at[span],
                dst_ref=g_v.at[span],
                send_sem=r.send_sem.at[batches + b],
                recv_sem=r.recv_sem.at[batches + b],
                device_id=sibling,
                device_id_type=MESH,
            )

        def spread(block):
            return jnp.concatenate([block] * heads, axis=0) * mask_v[...]

        def gathered(block):
            lane = lax.broadcasted_iota(jnp.int32, (latents, LANES), 1) // HEAD_DIM
            total = block[0:latents]
            for k in range(1, heads):
                total = jnp.where(lane == k, block[k * latents : (k + 1) * latents], total)
            return total

        def chains(i, local):
            for k in range(TOGETHER):
                at = pl.ds(pl.multiple_of((i + k) * latents, latents), latents)
                here = slice((local + k) * latents, (local + k + 1) * latents)
                for n in range(groups):
                    lanes = slice(n * LANES, (n + 1) * LANES)
                    values = slice(inner + n * LANES, inner + (n + 1) * LANES)
                    yield i + k, (i + k) * groups + n, at, here, lanes, values

        def attend(i):
            todo = list(chains(i, 0))
            scores = [
                dot_rows(kv_v[img, :, lanes], spread(q_v[at, lanes]))
                for img, _, at, _, lanes, _ in todo
            ]
            e = [jnp.exp(s - jnp.max(s, axis=0, keepdims=True)) for s in scores]
            prob = [(v * (1.0 / jnp.sum(v, axis=0, keepdims=True))).astype(BF16) for v in e]
            for (_, slot, *_), p in zip(todo, prob):
                p_v[slot] = p
            mixed = [dot_cols(p, kv_v[img, :, values]) for (img, *_, values), p in zip(todo, prob)]
            for (_, _, at, _, lanes, _), o in zip(todo, mixed):
                o_v[at, lanes] = gathered(o).astype(BF16)

        def attend_back(i, local):
            todo = list(chains(i, local))
            wide = [spread(do_v[here, lanes]) for _, _, _, here, lanes, _ in todo]
            dprob = [dot_rows(kv_v[c[0], :, c[5]], w) for c, w in zip(todo, wide)]
            dv = [dot(p_v[c[1]], w) for c, w in zip(todo, wide)]
            ds = []
            for c, d in zip(todo, dprob):
                p = p_v[c[1]].astype(F32)
                t = p * d
                ds.append((t - p * jnp.sum(t, axis=0, keepdims=True)).astype(BF16))
            query = [spread(q_v[at, lanes]) for _, _, at, _, lanes, _ in todo]
            dq = [dot_cols(d, kv_v[c[0], :, c[4]]) for c, d in zip(todo, ds)]
            dk = [dot(d, q) for d, q in zip(ds, query)]
            for (img, _, at, _, lanes, values), dq_, dk_, dv_ in zip(todo, dq, dk, dv):
                dq_v[at, lanes] = gathered(dq_).astype(BF16) * BF16(HEAD_DIM**-0.5)
                kv_v[img, :, lanes] = dk_.astype(BF16)
                kv_v[img, :, values] = dv_.astype(BF16)

        def forward(b, carry):
            span = pl.ds(pl.multiple_of(b * per, per), per)

            @pl.when(section == 1)
            def _():
                relay_latents(b).wait_recv()

            zed = z_v[span, :].astype(F32)
            hat, _ = normed(zed)
            low = (hat * r.latent_gain[...] + r.latent_bias[...]).astype(BF16)
            j_v[pl.ds(b * GROUP, GROUP), pl.ds(patches, latents), :] = low.reshape(
                GROUP, latents, width
            )
            q_v[span, :] = (dot(low, wq_v[...]) * HEAD_DIM**-0.5).astype(BF16)
            kv_v[pl.ds(b * GROUP, GROUP), pl.ds(patches, latents), :] = (
                dot(low, wkv_v[...]).astype(BF16).reshape(GROUP, latents, 2 * inner)
            )

            for k in range(0, GROUP, TOGETHER):
                attend(b * GROUP + k)
            mixed = zed + dot(o_v[span, :], wo_v[...])
            z1_v[span, :] = mixed
            hat, _ = normed(mixed)
            low = (hat * r.ff_gain[...] + r.ff_bias[...]).astype(BF16)
            f_v[span, :] = low
            if fused:
                exchange_f(b).start()
            u = dot(low, wu_v[:, 0:STEP])
            for c in range(chunks):
                lanes = slice(c * STEP, (c + 1) * STEP)
                later = None
                if c + 1 < chunks:
                    later = dot(low, wu_v[:, (c + 1) * STEP : (c + 2) * STEP])
                h, slope = gelu_and_slope(u)
                h = h.astype(BF16)
                h_v[c, span, :] = h
                sl_v[c, span, :] = slope.astype(BF16)
                part = dot(h, wd_v[lanes, :])
                acc[...] = part + (mixed if c == 0 else acc[...])
                u = later
            y_v[span, :] = acc[...].astype(BF16)

            @pl.when(section == 0)
            def _():
                relay_latents(b).start()

            if fused:
                @pl.when((section == 1) | (b + 1 < batches))
                def _():
                    exchange_h(b).start()

            return carry

        lax.fori_loop(0, batches, forward, 0)
        y_store = store(0, y_v, r.y_out)
        y_store.start()

        def backward_ff(b, carry):
            span = pl.ds(pl.multiple_of(b * per, per), per)

            @pl.when(section == 0)
            def _():
                if fused:

                    @pl.when(b == 0)
                    def _():
                        pl.semaphore_wait(r.go, 1)
                        exchange_h(batches - 1).start()

                relay_grad(b).wait_recv()
                if fused:
                    exchange_g(b).start()

            g = g_v[span, :]
            dh = dot_rows(g, wd_v[0:STEP, :])
            for c in range(chunks):
                lanes = slice(c * STEP, (c + 1) * STEP)
                later = None
                if c + 1 < chunks:
                    later = dot_rows(g, wd_v[(c + 1) * STEP : (c + 2) * STEP, :])
                du = (dh * sl_v[c, span, :].astype(F32)).astype(BF16)
                sl_v[c, span, :] = du
                part = dot_rows(du, wu_v[:, lanes])
                acc[...] = part if c == 0 else acc[...] + part
                dh = later
            if fused:
                exchange_u(b).start()

                @pl.when((section == 1) & (b == 0))
                def _():
                    signal(r.go, sibling)

            df = acc[...]
            hat, factor = normed(z1_v[span, :])
            r.lines[4:5, :] += jnp.sum(df * hat, axis=0, keepdims=True)
            r.lines[5:6, :] += jnp.sum(df, axis=0, keepdims=True)
            dz1 = g.astype(F32) + norm_back(df, hat, factor, r.ff_gain[...])
            z1_v[span, :] = dz1
            dz1_v[span, :] = dz1.astype(BF16)
            return carry

        lax.fori_loop(0, batches, backward_ff, 0)
        y_store.wait()

        @pl.when(section == 0)
        def _():
            for b in range(batches):
                relay_latents(b).wait_send()

        def backward_attention(b, carry):
            span = pl.ds(pl.multiple_of(b * per, per), per)
            do_v[...] = dot_rows(dz1_v[span, :], wo_v[...]).astype(BF16)

            for k in range(0, GROUP, TOGETHER):
                attend_back(b * GROUP + k, k)
            tail = kv_v[pl.ds(b * GROUP, GROUP), pl.ds(patches, latents), :].reshape(per, 2 * inner)
            dn = dot_rows(dq_v[span, :], wq_v[...]) + dot_rows(tail, wkv_v[...])
            hat, factor = normed(z_v[span, :].astype(F32))
            r.lines[2:3, :] += jnp.sum(dn * hat, axis=0, keepdims=True)
            r.lines[3:4, :] += jnp.sum(dn, axis=0, keepdims=True)
            dz = z1_v[span, :] + norm_back(dn, hat, factor, r.latent_gain[...])
            y_v[span, :] = dz.astype(BF16)

            @pl.when(section == 1)
            def _():
                relay_grad(b).start()

            @pl.when(section == 0)
            def _():
                total = dz[0:latents]
                for k in range(1, GROUP):
                    total = total + dz[k * latents : (k + 1) * latents]
                r.lines[8 : 8 + latents, :] += total

            return carry

        lax.fori_loop(0, batches, backward_attention, 0)

        @pl.when(section == 1)
        def _():
            for b in range(batches):
                relay_grad(b).wait_send()

    pl.run_scoped(
        phase_one,
        pltpu.VMEM(r.wq.shape, BF16),
        pltpu.VMEM(r.wo.shape, BF16),
        pltpu.VMEM(r.wu.shape, BF16),
        pltpu.VMEM(r.wd.shape, BF16),
        pltpu.VMEM((rows, width), BF16),
        pltpu.VMEM((rows, inner), BF16),
        pltpu.VMEM((images * groups, patches + latents, heads * latents), BF16),
        pltpu.VMEM((rows, width), F32),
        pltpu.VMEM((rows, width), BF16),
        pltpu.VMEM((per, width), F32),
        pltpu.VMEM((per, inner), BF16),
        pltpu.VMEM((heads * latents, LANES), BF16),
    )

    if not fused:
        copies = [
            store(k + 1, src, dst)
            for k, (src, dst) in enumerate(
                [
                    (j_v, r.j_out),
                    (kv_v, r.kv_out),
                    (o_v, r.o_out),
                    (f_v, r.f_out),
                    (h_v, r.h_out),
                    (sl_v, r.du_out),
                    (dz1_v, r.dz1_out),
                    (dq_v, r.dq_out),
                    (g_v, r.g_out),
                ]
            )
        ]
        for copy in copies:
            copy.start()
        for copy in copies:
            copy.wait()
        r.lines_out[...] = r.lines[...]
        return


    def z_base(kind, c):
        return first_of(kind, c) if order_of(kind, c) == "zx" else second_of(kind, c)

    def up_copy(kind, c, d, src):
        return remote(kind, c, 2 + d, src, z_of(kind, c).at[d], at_up)

    def down_copy(kind, c, d, src, last):
        place = 4 if last else d
        return remote(kind, c, 2 + place, src, z_of(kind, c).at[place], at_down)

    def add_into(dst, src):
        lead = dst.shape[:-2]
        if not lead:
            dst[...] = halves(dst[...], src[...])
            return
        total = 1
        for size in lead:
            total *= size

        def step(k, carry):
            at = []
            for size in reversed(lead):
                at.append(lax.rem(k, size))
                k = k // size
            at = tuple(reversed(at))
            dst[at] = halves(dst[at], src[at])
            return carry

        lax.fori_loop(0, total, step, 0)

    def send_own(kind, c, d, up):
        src = z_base(kind, c).at[d]
        if up:
            up_copy(kind, c, d, src).start()
        else:
            down_copy(kind, c, d, src, d == 2).start()

    def pass_on(kind, c, d, up, last=False):
        zb = z_of(kind, c)
        up_copy(kind, c, d, zb.at[d]).wait_recv()
        add_into(zb.at[d], z_base(kind, c).at[d])
        if up:
            up_copy(kind, c, d, zb.at[d]).start()
        else:
            down_copy(kind, c, d, zb.at[d], last).start()

    def z_start(kind, c):
        zb = z_of(kind, c)

        @pl.when(z == 0)
        def _():
            zb[0] = jnp.zeros(zb.shape[1:], zb.dtype)
            send_own(kind, c, 3, True)

        @pl.when(z == 3)
        def _():
            zb[4] = jnp.zeros(zb.shape[1:], zb.dtype)
            send_own(kind, c, 0, False)

    def z_near(kind, c):
        @pl.when(z == 0)
        def _():
            send_own(kind, c, 2, True)

        @pl.when(z == 1)
        def _():
            pass_on(kind, c, 3, True)

        @pl.when(z == 2)
        def _():
            pass_on(kind, c, 0, False)

        @pl.when(z == 3)
        def _():
            send_own(kind, c, 1, False)

    def z_far(kind, c):
        @pl.when(z == 0)
        def _():
            send_own(kind, c, 1, True)

        @pl.when(z == 1)
        def _():
            pass_on(kind, c, 0, False, True)
            pass_on(kind, c, 2, True)

        @pl.when(z == 2)
        def _():
            pass_on(kind, c, 3, True)
            pass_on(kind, c, 1, False, True)

        @pl.when(z == 3)
        def _():
            send_own(kind, c, 2, False)

    def z_arrive(kind, c):
        zb = z_of(kind, c)

        @pl.when(z > 0)
        def _():
            remote(kind, c, 2 + z, zb.at[z], zb.at[z], at_up).wait_recv()

        @pl.when(z < 3)
        def _():
            remote(kind, c, 6, zb.at[4], zb.at[4], at_down).wait_recv()

    def finish(kind, c, total):
        def put(k, rows_at, lanes_at, value):
            held, out = results()[k]
            held[rows_at, lanes_at] = value
            out_copy(held.at[rows_at, lanes_at], out.at[rows_at, lanes_at], k).start()

        tall = total.shape[0]
        if kind == DOWN:
            rows_at, lanes_at = down_at(c)
            put(1, rows_at, lanes_at, total)
        elif kind == ATT and c < 2:
            put(2, slice(0, tall), slice(c * LANES, (c + 1) * LANES), total)
        elif kind == ATT and c < 4:
            tall = tall // 2
            for n in range(2):
                at = ((c - 2) * 2 + n) * LANES
                value = total[n * tall : (n + 1) * tall]
                put(3, slice(0, tall), slice(at, at + LANES), value)
        elif kind == ATT:
            at = (c - 4) * LANES
            put(4, slice(0, tall), slice(at, at + LANES), total)
        else:
            r.small_out[...] = total

            @pl.when(section == 0)
            def _():
                relay_start().start()
                own_start().start()

    def relay_start():
        last = 2 * batches + images
        return pltpu.make_async_remote_copy(
            src_ref=r.small_out,
            dst_ref=r.start_out,
            send_sem=r.send_sem.at[last],
            recv_sem=r.recv_sem.at[last],
            device_id=sibling,
            device_id_type=MESH,
        )

    def own_start():
        return store(9, r.small_out, r.start_out)

    def results():
        return (
            (r.up_out, r.up_out),
            (r.down_v, r.down_out),
            (r.query_v, r.query_out),
            (r.out_v, r.out_out),
            (r.keyval_v, r.keyval_out),
        )

    def out_copy(src, dst, k):
        return pltpu.make_async_copy(src, dst, r.out_sem.at[k])

    def down_at(c):
        tall = hidden // 32
        return slice(c // 4 * tall, (c // 4 + 1) * tall), slice(c % 4 * LANES, (c % 4 + 1) * LANES)

    def put_up(c, n, half, total):
        held = r.up_v.at[n, :, pl.ds(c * LANES, LANES)]
        held[...] = total
        at = pl.multiple_of(half * (hidden // 2) + c * LANES, LANES)
        out_copy(held, r.up_out.at[:, pl.ds(at, LANES)], 0).start()

    def advance(kind, c, step):
        zb = z_of(kind, c)
        if kind == DOWN and c < DOWN_Z:
            base = first_of(kind, c)
            if step == 1:
                z_near(kind, c)
            elif step == 2:
                z_far(kind, c)
            elif step == 3:
                z_arrive(kind, c)
                total = base[z, 1 - x].astype(F32) + zb[z, 1 - x].astype(F32)
                zb[z, 1 - x] = (total + zb[4, 1 - x].astype(F32)).astype(BF16)
                end_copy(kind, c).start()
                total = base[z, x].astype(F32) + zb[z, x].astype(F32)
                r.down_v[down_at(c)] = total + zb[4, x].astype(F32)
            elif step == 4:
                end_copy(kind, c).wait_recv()
                finish(kind, c, r.down_v[down_at(c)] + r.end_d[c].astype(F32))
            return
        order = order_of(kind, c)
        first, second = first_of(kind, c), second_of(kind, c)
        if step == 1:
            base = base_of(kind, c)
            first_copy(kind, c).wait_recv()
            add_into(first, base.at[:, :, x] if order == "xyz" else base.at[:, y])
            second_copy(kind, c).start()
        elif step == 2:
            second_copy(kind, c).wait_recv()
            add_into(second, first.at[:, y] if order == "xyz" else first.at[:, x])
            z_start(kind, c)
        elif step == 3:
            z_near(kind, c)
        elif step == 4:
            z_far(kind, c)
        elif step == 5 and kind == UP:
            z_arrive(kind, c)
            total = second[z, 1 - x].astype(F32) + zb[z, 1 - x].astype(F32)
            r.end_src[c] = (total + zb[4, 1 - x].astype(F32)).astype(BF16)
            end_copy(kind, c).start()
            total = second[z, x].astype(F32) + zb[z, x].astype(F32)
            put_up(c, 0, x, total + zb[4, x].astype(F32))
        elif step == 5:
            z_arrive(kind, c)
            total = second[z].astype(F32) + zb[z].astype(F32)
            finish(kind, c, total + zb[4].astype(F32))
        elif step == 6 and kind == UP:
            end_copy(kind, c).wait_recv()
            put_up(c, 1, 1 - x, r.end_u[c].astype(F32))

    def sends_done():
        for kind, c in BLOCKS:
            taken = 0 <= 2 * c - before(kind, c) < CHUNKS
            if kind == SMALL or (kind == ATT and not taken):
                first_copy(kind, c).wait_send()
            if not (kind == DOWN and c < DOWN_Z) and not (kind == UP and taken):
                second_copy(kind, c).wait_send()
            if kind == UP or (kind == DOWN and c < DOWN_Z):
                end_copy(kind, c).wait_send()
        for kind, along in (
            (UP, r.z_u),
            (DOWN, r.z_d),
            (DOWN, r.z_d_late),
            (ATT, r.z_a),
            (SMALL, r.z_s),
        ):
            along = along.at[0:3] if kind == SMALL else along.at[:, 0:3]
            remote(kind, 0, 2, along, along, at_x).wait_send()
        for b in range(batches):
            for copy in (exchange_f(b), exchange_u(b), exchange_g(b), exchange_h(b)):
                copy.wait_send()

    def phase_two(*buffers):
        names_two = ["first_u", "second_u", "z_u", "end_src", "end_u", "first_d"]
        names_two += ["second_d", "z_d", "z_d_late", "end_d"]
        names_two += ["base_a", "first_a", "second_a", "z_a"]
        names_two += ["base_s", "first_s", "second_s", "z_s", "media_v", "mine_v", "other_v"]
        names_two += ["up_v", "down_v", "keyval_v", "query_v", "out_v"]
        r.__dict__.update(zip(names_two, buffers, strict=True))
        media_v, mine_v, other_v = r.media_v, r.mine_v, r.other_v

        signal(r.ready.at[0], at_x)
        signal(r.ready.at[1], at_y)

        @pl.when(z < 3)
        def _():
            signal(r.ready.at[2], at_up)

        @pl.when(z > 0)
        def _():
            signal(r.ready.at[3], at_down)

        def urgency(entry):
            step, kind, c = entry
            return step == final(kind, c), step - final(kind, c), kind, c

        def image_load(i):
            return load(6 + i, r.media.at[i], media_v.at[i % 2])

        def mine_store(i):
            return store(1 + i, mine_v, r.mine_out.at[i])

        def relay_media(i):
            return pltpu.make_async_remote_copy(
                src_ref=other_v.at[i % 2],
                dst_ref=r.theirs_out.at[i],
                send_sem=r.send_sem.at[2 * batches + i],
                recv_sem=r.recv_sem.at[2 * batches + i],
                device_id=sibling,
                device_id_type=MESH,
            )

        def media_grad(i):
            half = width // 2
            image_load(i).wait()
            dj = dot_rows(kv_v[i, pl.ds(0, patches), :], wkv_v[...])
            hat, factor = normed(media_v[i % 2].astype(F32))
            r.lines[0:1, :] += jnp.sum(dj * hat, axis=0, keepdims=True)
            r.lines[1:2, :] += jnp.sum(dj, axis=0, keepdims=True)
            grad = norm_back(dj, hat, factor, r.media_gain[...])
            if i >= 1:
                mine_store(i - 1).wait()
            if i >= 2:
                relay_media(i - 2).wait_send()

            @pl.when(section == 0)
            def _():
                mine_v[...] = grad[:, :half]
                other_v[i % 2] = grad[:, half:].astype(BF16)

            @pl.when(section == 1)
            def _():
                mine_v[...] = grad[:, half:]
                other_v[i % 2] = grad[:, :half].astype(BF16)

            mine_store(i).start()
            relay_media(i).start()
            if i + 2 < images:
                image_load(i + 2).start()

        image_load(0).start()
        image_load(1).start()
        pl.semaphore_wait(r.ready.at[0], 1)
        pl.semaphore_wait(r.ready.at[1], 1)

        @pl.when(z > 0)
        def _():
            pl.semaphore_wait(r.ready.at[2], 1)

        @pl.when(z < 3)
        def _():
            pl.semaphore_wait(r.ready.at[3], 1)

        slots = {(SMALL, 0): SMALL_SLOT}
        for kind, at in ((DOWN, DOWN_SLOTS), (ATT, ATT_SLOTS), (UP, UP_SLOTS)):
            slots.update({(kind, c): slot for c, slot in enumerate(at)})
        last = max(slots.values()) + 7
        for b in range(batches):
            exchange_g(b).wait_recv()
            exchange_h(b).wait_recv()

        def final(kind, c):
            return 6 if kind == UP else 4 if kind == DOWN and c < DOWN_Z else 5

        def slot_of(kind, c, step):
            return slots[kind, c] + step - paired(kind, c)

        for slot in range(last):
            for (kind, c), at in slots.items():
                if at == slot and c % 2 == 0:
                    if kind == UP and c == 0:
                        for b in range(batches):
                            exchange_f(b).wait_recv()
                            exchange_u(b).wait_recv()
                    begin(kind, c)
            live = []
            for kind, c in slots:
                steps = range(1 + paired(kind, c), final(kind, c) + 1)
                live += [(n, kind, c) for n in steps if slot_of(kind, c, n) == slot]
            for step, kind, c in sorted(live, key=urgency):
                advance(kind, c, step)
            for i in range(images):
                if MEDIA_SLOTS[i] == slot:
                    media_grad(i)

        sends_done()
        mine_store(images - 1).wait()
        for i in range(images - 2, images):
            relay_media(i).wait_send()
        for i in range(images):
            relay_media(i).wait_recv()
        for k, (held, out) in enumerate(results()):
            out_copy(held, out, k).wait()

        @pl.when(section == 0)
        def _():
            relay_start().wait_send()
            own_start().wait()

        @pl.when(section == 1)
        def _():
            relay_start().wait_recv()

    tile_u, tile_d = (width // 16, LANES), (hidden // 32, LANES)
    tile_a, tile_s = (width // 16, LANES), (40, 128)
    pl.run_scoped(
        phase_two,
        pltpu.VMEM((RING, 4, 2, 2) + tile_u, BF16),
        pltpu.VMEM((CHUNKS, 4, 2) + tile_u, BF16),
        pltpu.VMEM((CHUNKS, 5, 2) + tile_u, BF16),
        pltpu.VMEM((CHUNKS,) + tile_u, BF16),
        pltpu.VMEM((CHUNKS,) + tile_u, BF16),
        pltpu.VMEM((CHUNKS, 4, 2) + tile_d, BF16),
        pltpu.VMEM((CHUNKS - DOWN_Z, 4) + tile_d, BF16),
        pltpu.VMEM((DOWN_Z, 5, 2) + tile_d, BF16),
        pltpu.VMEM((CHUNKS - DOWN_Z, 5) + tile_d, BF16),
        pltpu.VMEM((DOWN_Z,) + tile_d, BF16),
        pltpu.VMEM((RING, 4, 2, 2) + tile_a, BF16),
        pltpu.VMEM((CHUNKS, 4, 2) + tile_a, BF16),
        pltpu.VMEM((CHUNKS, 4) + tile_a, BF16),
        pltpu.VMEM((CHUNKS, 5) + tile_a, BF16),
        pltpu.VMEM((4, 2, 2) + tile_s, F32),
        pltpu.VMEM((4, 2) + tile_s, F32),
        pltpu.VMEM((4,) + tile_s, F32),
        pltpu.VMEM((5,) + tile_s, F32),
        pltpu.VMEM((2, patches, width), BF16),
        pltpu.VMEM((patches, width // 2), F32),
        pltpu.VMEM((2, patches, width // 2), BF16),
        pltpu.VMEM((2, width // 16, hidden // 2), F32),
        pltpu.VMEM((hidden // 16, width), F32),
        pltpu.VMEM((width // 16, 2 * inner), F32),
        pltpu.VMEM((width // 16, inner), F32),
        pltpu.VMEM((inner // 16, width), F32),
    )


def layers(fused, start, media, cotangent, live, lines, wq, wkv, wo, wu, wd):
    images, patches, width = media.shape
    latents = start.shape[0]
    inner = wq.shape[1]
    hidden = wu.shape[1]
    rows = images * latents
    batches = images // GROUP
    dims = (images, latents, patches, inner, hidden, width)
    keys = patches + latents
    any_spec = pl.BlockSpec(memory_space=pl.ANY)
    vmem_spec = pl.BlockSpec(memory_space=pltpu.VMEM)
    smem_spec = pl.BlockSpec(memory_space=pltpu.SMEM)

    def low(*shape):
        return jax.ShapeDtypeStruct(shape, BF16)

    def full(*shape):
        return jax.ShapeDtypeStruct(shape, F32)

    ins = [
        ("start", start, any_spec),
        ("media", media, any_spec),
        ("cotangent", cotangent, any_spec),
        ("live", live, smem_spec),
    ]
    line_names = ["media_gain", "media_bias", "latent_gain", "latent_bias", "ff_gain", "ff_bias"]
    ins += [(n, a, vmem_spec) for n, a in zip(line_names, lines, strict=True)]
    ins += [(n, a, any_spec) for n, a in zip(("wq", "wkv", "wo", "wu", "wd"), (wq, wkv, wo, wu, wd))]
    outs = [("y_out", low(rows, width), any_spec)]
    if fused:
        outs += [
            ("mine_out", full(images, patches, width // 2), any_spec),
            ("theirs_out", low(images, patches, width // 2), any_spec),
            ("up_out", full(width // 16, hidden), any_spec),
            ("down_out", full(hidden // 16, width), any_spec),
            ("keyval_out", full(width // 16, 2 * inner), any_spec),
            ("query_out", full(width // 16, inner), any_spec),
            ("out_out", full(inner // 16, width), any_spec),
            ("start_out", full(40, 128), any_spec),
            ("small_out", full(40, 128), vmem_spec),
        ]
    else:
        outs += [
            ("j_out", low(images, keys, width), any_spec),
            ("kv_out", low(images, keys, 2 * inner), any_spec),
            ("o_out", low(rows, inner), any_spec),
            ("f_out", low(rows, width), any_spec),
            ("h_out", low(hidden // STEP, rows, STEP), any_spec),
            ("du_out", low(hidden // STEP, rows, STEP), any_spec),
            ("dz1_out", low(rows, width), any_spec),
            ("dq_out", low(rows, inner), any_spec),
            ("g_out", low(rows, width), any_spec),
            ("lines_out", full(80, width), vmem_spec),
        ]
    scratch = [
        ("wkv_v", pltpu.VMEM(wkv.shape, BF16)),
        ("j_v", pltpu.VMEM((images, keys, width), BF16)),
        ("kv_v", pltpu.VMEM((images, keys, 2 * inner), BF16)),
        ("o_v", pltpu.VMEM((rows, inner), BF16)),
        ("f_v", pltpu.VMEM((rows, width), BF16)),
        ("h_v", pltpu.VMEM((hidden // STEP, rows, STEP), BF16)),
        ("sl_v", pltpu.VMEM((hidden // STEP, rows, STEP), BF16)),
        ("g_v", pltpu.VMEM((rows, width), BF16)),
        ("dz1_v", pltpu.VMEM((rows, width), BF16)),
        ("dq_v", pltpu.VMEM((rows, inner), BF16)),
        ("lines", pltpu.VMEM((80, width), F32)),
        ("load_sem", pltpu.SemaphoreType.DMA((7 + images,))),
        ("store_sem", pltpu.SemaphoreType.DMA((10,))),
        ("send_sem", pltpu.SemaphoreType.DMA((2 * batches + images + 1,))),
        ("recv_sem", pltpu.SemaphoreType.DMA((2 * batches + images + 1,))),
    ]
    if fused:
        scratch += [
            ("hn_v", pltpu.VMEM((4, rows, STEP), BF16)),
            ("gn_v", pltpu.VMEM((rows, width), BF16)),
            ("fn_v", pltpu.VMEM((rows, width), BF16)),
            ("un_v", pltpu.VMEM((4, rows, STEP), BF16)),
            ("pair_send", pltpu.SemaphoreType.DMA((4, batches))),
            ("pair_recv", pltpu.SemaphoreType.DMA((4, batches))),
            ("rs_send", pltpu.SemaphoreType.DMA((2 * len(BLOCKS) + 5,))),
            ("rs_recv", pltpu.SemaphoreType.DMA((len(BLOCKS), 8))),
            ("out_sem", pltpu.SemaphoreType.DMA((5,))),
            ("go", pltpu.SemaphoreType.REGULAR),
            ("ready", pltpu.SemaphoreType.REGULAR((4,))),
        ]
    names = [n for n, *_ in ins] + [n for n, *_ in outs] + [n for n, _ in scratch]
    results = pl.pallas_call(
        functools.partial(layer_kernel, dims, fused, names),
        out_shape=[s for _, s, _ in outs],
        in_specs=[s for _, _, s in ins],
        out_specs=[s for _, _, s in outs],
        scratch_shapes=[s for _, s in scratch],
        compiler_params=pltpu.CompilerParams(
            collective_id=1, has_side_effects=True, vmem_limit_bytes=VMEM_LIMIT
        ),
        name="layers",
    )(*[a for _, a, _ in ins])
    return Refs([n for n, *_ in outs], results)


def media_kernel(dims, dkv, media, wkv, gain, mine, other, sums):
    patches, half = dims
    section = lax.axis_index("section")

    @pl.when(pl.program_id(0) == 0)
    def _():
        sums[...] = jnp.zeros_like(sums)

    dj = dot_rows(dkv[0], wkv[...])
    hat, factor = normed(media[0].astype(F32))
    sums[0:1, :] += jnp.sum(dj * hat, axis=0, keepdims=True)
    sums[1:2, :] += jnp.sum(dj, axis=0, keepdims=True)
    grad = norm_back(dj, hat, factor, gain[...])

    @pl.when(section == 0)
    def _():
        mine[0] = grad[:, :half]
        other[0] = grad[:, half:].astype(BF16)

    @pl.when(section == 1)
    def _():
        mine[0] = grad[:, half:]
        other[0] = grad[:, :half].astype(BF16)


def media_grads(dkv, media, wkv, gain):
    images, patches, width = media.shape
    half = width // 2
    return pl.pallas_call(
        functools.partial(media_kernel, (patches, half)),
        grid=(images,),
        out_shape=[
            jax.ShapeDtypeStruct((images, patches, half), F32),
            jax.ShapeDtypeStruct((images, patches, half), BF16),
            jax.ShapeDtypeStruct((8, width), F32),
        ],
        in_specs=[
            pl.BlockSpec((1, patches, dkv.shape[2]), lambda i: (i, 0, 0)),
            pl.BlockSpec((1, patches, width), lambda i: (i, 0, 0)),
            pl.BlockSpec(wkv.shape, lambda i: (0, 0)),
            pl.BlockSpec((1, width), lambda i: (0, 0)),
        ],
        out_specs=[
            pl.BlockSpec((1, patches, half), lambda i: (i, 0, 0)),
            pl.BlockSpec((1, patches, half), lambda i: (i, 0, 0)),
            pl.BlockSpec((8, width), lambda i: (0, 0)),
        ],
        compiler_params=pltpu.CompilerParams(vmem_limit_bytes=48 * 1024 * 1024),
        name="media_grads",
    )(dkv, media, wkv, gain)


def hand_over_kernel(latents, mine, theirs, small, start, *refs):
    count = (len(refs) - 8) // 2
    sources, media_out, start_out = refs[:count], refs[count], refs[count + 1]
    lines, targets = refs[count + 2 : count + 8], refs[count + 8 :]
    section = lax.axis_index("section")

    @pl.when(pl.program_id(0) == 0)
    def _():
        for k, line in enumerate(lines):
            line[...] = small[k : k + 1, :64]

        @pl.when(section == 0)
        def _():
            start_out[...] = start[8 : 8 + latents // 2, :64]

        @pl.when(section == 1)
        def _():
            start_out[...] = start[: latents // 2, 64:]

    media_out[...] = mine[...] + theirs[...].astype(F32)
    for source, target in zip(sources, targets):
        target[...] = source[...]


def hand_over(latents, mine, theirs, small, start, arrays):
    images, patches, half = mine.shape
    steps = 4
    media_spec = pl.BlockSpec((images // steps, patches, half), lambda i: (i, 0, 0))

    def whole(shape):
        return pl.BlockSpec(shape, lambda i: (0, 0))

    line, start_shape = (1, 64), (latents // 2, 64)
    parts = [pl.BlockSpec((a.shape[0] // steps, a.shape[1]), lambda i: (i, 0)) for a in arrays]
    return pl.pallas_call(
        functools.partial(hand_over_kernel, latents),
        grid=(steps,),
        out_shape=[jax.ShapeDtypeStruct(mine.shape, F32), jax.ShapeDtypeStruct(start_shape, F32)]
        + [jax.ShapeDtypeStruct(line, F32)] * 6
        + [jax.ShapeDtypeStruct(a.shape, a.dtype) for a in arrays],
        in_specs=[media_spec, media_spec, whole(small.shape), whole(start.shape)] + parts,
        out_specs=[media_spec, whole(start_shape)] + [whole(line)] * 6 + parts,
        compiler_params=pltpu.CompilerParams(vmem_limit_bytes=VMEM_LIMIT),
        name="hand_over",
    )(mine, theirs, small, start, *arrays)


def weight_grad(left, right):
    left = left.reshape(-1, left.shape[-1])
    right = right.reshape(-1, right.shape[-1])
    return dot_cols(left, right).astype(BF16)


def swap_sections(value):
    return lax.ppermute(value, "section", [(0, 1), (1, 0)])


def shards(
    media,
    image_live,
    start_latents,
    latent_cotangent,
    media_gain,
    media_bias,
    latent_gain,
    latent_bias,
    w_query,
    w_kv,
    w_out,
    ff_gain,
    ff_bias,
    w_up,
    w_down,
):
    images, patches, width = media.shape
    latents = start_latents.shape[0]
    peers = lax.axis_size("dp")
    rows = images * latents
    fused = peers == 16
    wkv = w_kv[0]
    k = layers(
        fused,
        start_latents,
        media,
        latent_cotangent.reshape(rows, width),
        image_live,
        (media_gain, media_bias, latent_gain, latent_bias, ff_gain, ff_bias),
        w_query[0],
        wkv,
        w_out[0],
        w_up[0],
        w_down[0],
    )
    if fused:
        media_grad, start_grad, *rest = hand_over(
            latents,
            k.mine_out,
            k.theirs_out,
            k.small_out,
            k.start_out,
            [k.y_out, k.query_out, k.keyval_out, k.out_out, k.up_out, k.down_out],
        )
        lines = rest[:6]
        y_low, query, kv, out, up, down = rest[6:]
    else:
        mine, other, media_sums = media_grads(k.kv_out, media, wkv, media_gain)
        theirs = swap_sections(other)
        up, down, kv, query, out = (
            lax.psum_scatter(a, "dp", scatter_dimension=0, tiled=True).astype(F32)
            for a in (
                weight_grad(k.f_out, k.du_out.swapaxes(0, 1).reshape(rows, -1)),
                weight_grad(k.h_out.swapaxes(0, 1).reshape(rows, -1), k.g_out),
                weight_grad(k.j_out, k.kv_out),
                weight_grad(k.j_out[:, patches:], k.dq_out),
                weight_grad(k.o_out, k.dz1_out),
            )
        )
        y_low = k.y_out
        lines = jnp.concatenate([media_sums[:2], k.lines_out[2:6]], axis=0)
        lines = lax.psum_scatter(lines, "dp", scatter_dimension=1, tiled=True)
        lines = jnp.split(lines, 6, axis=0)
        start_part = lax.psum_scatter(
            k.lines_out[8 : 8 + latents], "dp", scatter_dimension=1, tiled=True
        )
        half = latents // 2
        far = swap_sections(start_part[half:])
        start_grad = jnp.where(lax.axis_index("section") == 0, start_part[:half], far)
        media_grad = mine + theirs.astype(F32)
    return (
        y_low.reshape(1, images, latents, width),
        media_grad,
        start_grad,
        *lines[:4],
        query[None],
        kv[None],
        out[None],
        *lines[4:],
        up[None],
        down[None],
    )


def solution(mesh):
    row = P("section", None)
    mat = P("section", None, None)
    in_specs = (
        P("dp", None, None), P("dp"), P(), P("dp", None, None),
        row, row, row, row, mat, mat, mat, row, row, mat, mat,
    )
    line = P("section", "dp")
    block = P("section", "dp", None)
    out_specs = (
        P("section", "dp", None, None), P("dp", None, "section"), line,
        line, line, line, line, block, block, block, line, line, block, block,
    )
    return jax.shard_map(shards, mesh=mesh, in_specs=in_specs, out_specs=out_specs, check_vma=False)
```

```python
import functools

import jax
import jax.numpy as jnp
from jax import lax
from jax.experimental import pallas as pl
from jax.experimental.pallas import tpu as pltpu
from jax.sharding import PartitionSpec as P

MESH = pl.DeviceIdType.MESH
F32 = jnp.float32
BF16 = jnp.bfloat16
HEAD_DIM = 64
LANES = 256
GROUP = 4
TOGETHER = 4
STEP = 512
VMEM_LIMIT = 63 * 1024 * 1024


def dot(left, right):
    return jnp.dot(left, right, preferred_element_type=F32)


def dot_rows(left, right):
    return lax.dot_general(left, right, (((1,), (1,)), ((), ())), preferred_element_type=F32)


def dot_cols(left, right):
    return lax.dot_general(left, right, (((0,), (0,)), ((), ())), preferred_element_type=F32)


def normed(value):
    centred = value - jnp.mean(value, axis=-1, keepdims=True)
    factor = lax.rsqrt(jnp.mean(centred * centred, axis=-1, keepdims=True) + 1e-05)
    return centred * factor, factor


def norm_back(upstream, hat, factor, gain):
    scaled = upstream * gain
    return factor * (
        scaled
        - jnp.mean(scaled, axis=-1, keepdims=True)
        - hat * jnp.mean(scaled * hat, axis=-1, keepdims=True)
    )


def gelu_and_slope(u):
    e = jnp.exp2((u * u) * (-0.5 * 1.4426950408889634))
    t = pl.reciprocal(1.0 + jnp.abs(u) * (0.3275911 * 0.7071067811865476), approx=True)
    tail = t * (
        0.127414796 + t * (-0.142248368 + t * (0.7107068705 + t * (-0.7265760135 + t * 0.5307027145)))
    )
    tail = tail * e
    phi = jnp.where(u >= 0.0, 1.0 - tail, tail)
    return u * phi, phi + (u * e) * 0.3989422804014327


def halves(a, b):
    return (a.astype(F32) + b.astype(F32)).astype(a.dtype)


class Refs:
    def __init__(self, names, refs):
        self.__dict__.update(zip(names, refs, strict=True))


UP, DOWN, ATT, SMALL = 0, 1, 2, 3
CHUNKS = 8
RING = 4
DOWN_Z = 4
DOWN_SLOTS = (0, 0, 1, 1, 3, 3, 4, 4)
UP_SLOTS = (2, 2, 3, 3, 4, 4, 5, 5)
ATT_SLOTS = (5, 5, 6, 6, 3, 3, 4, 4)
MEDIA_SLOTS = (0, 0, 1, 1, 2, 3, 4, 4)
SMALL_SLOT = 5
BLOCKS = [(kind, c) for kind in (UP, DOWN, ATT) for c in range(CHUNKS)] + [(SMALL, 0)]


def layer_kernel(dims, fused, names, *all_refs):
    images, latents, patches, inner, hidden, width = dims
    r = Refs(names, all_refs)
    rows = images * latents
    per = GROUP * latents
    batches = images // GROUP
    groups = inner // LANES
    heads = LANES // HEAD_DIM
    chunks = hidden // STEP
    section = lax.axis_index("section")
    dp = lax.axis_index("dp")
    sibling = (1 - section, dp)
    x = lax.rem(dp, 2)
    y = lax.rem(dp // 2, 2)
    z = dp // 4
    at_x = (section, dp + 1 - 2 * x)
    at_y = (section, dp + 2 - 4 * y)
    at_up = (section, dp + 4)
    at_down = (section, dp - 4)
    j_v, kv_v, o_v, f_v, h_v, sl_v = r.j_v, r.kv_v, r.o_v, r.f_v, r.h_v, r.sl_v
    g_v, dz1_v, dq_v, wkv_v = r.g_v, r.dz1_v, r.dq_v, r.wkv_v

    def signal(sem, where):
        pl.semaphore_signal(sem, inc=1, device_id=where, device_id_type=MESH)

    def load(k, src, dst):
        return pltpu.make_async_copy(src, dst, r.load_sem.at[k])

    def store(k, src, dst):
        return pltpu.make_async_copy(src, dst, r.store_sem.at[k])

    def media_load(i):
        return load(6 + i, r.media.at[i], j_v.at[i, pl.ds(0, patches)])

    barrier = pltpu.get_barrier_semaphore()

    def greet():
        signal(barrier, sibling)
        if fused:
            signal(barrier, at_x)
            signal(barrier, at_y)

            @pl.when(z < 3)
            def _():
                signal(barrier, at_up)

            @pl.when(z > 0)
            def _():
                signal(barrier, at_down)

    def met():
        peers = 1
        if fused:
            peers = 3 + jnp.where(z < 3, 1, 0) + jnp.where(z > 0, 1, 0)
        pl.semaphore_wait(barrier, peers)


    def remote(kind, c, slot, src, dst, where):
        sem = sem_of(kind, c)
        along = not isinstance(slot, int) or 2 <= slot < 7
        sent = 2 * len(BLOCKS) + kind if along else sem + (len(BLOCKS) if slot == 1 else 0)
        return pltpu.make_async_remote_copy(
            src_ref=src,
            dst_ref=dst,
            send_sem=r.rs_send.at[sent],
            recv_sem=r.rs_recv.at[sem, slot],
            device_id=where,
            device_id_type=MESH,
        )

    def sem_of(kind, c):
        return BLOCKS.index((kind, c))

    def base_of(kind, c):
        return r.base_a.at[c % RING] if kind == ATT else r.base_s

    def before(kind, c):
        return (c - RING) if ATT_SLOTS[0] < ATT_SLOTS[RING] or kind == UP else (c + RING)

    def order_of(kind, c):
        if kind == DOWN:
            return "zx" if c < DOWN_Z else "yxz"
        return "yxz" if kind == ATT and c >= 2 else "xyz"

    def ordered(kind, c, act):
        if kind != ATT or c < 4:
            act(order_of(kind, c))
            return

        @pl.when(section == 0)
        def _():
            act("xyz")

        @pl.when(section == 1)
        def _():
            act("yxz")

    def first_of(kind, c):
        if kind == SMALL:
            return r.first_s
        return {UP: r.first_u.at[c % RING], DOWN: r.first_d.at[c], ATT: r.first_a.at[c]}[kind]

    def second_of(kind, c):
        if kind == DOWN:
            return r.second_d.at[c - DOWN_Z]
        return r.second_s if kind == SMALL else {UP: r.second_u, ATT: r.second_a}[kind].at[c]

    def z_of(kind, c):
        if kind == DOWN:
            return r.z_d.at[c] if c < DOWN_Z else r.z_d_late.at[c - DOWN_Z]
        return r.z_s if kind == SMALL else {UP: r.z_u, ATT: r.z_a}[kind].at[c]

    def paired(kind, c):
        return kind == UP or (kind == DOWN and c >= DOWN_Z)

    def compute(kind, c):
        both = [c, c + 1]
        if kind in (UP, DOWN):
            if kind == UP:
                part = dot_cols(f_v[...], sl_v[4 * x + c // 2])
                part = part + dot_cols(r.fn_v[...], r.un_v[c // 2])
            else:
                side, q = c // 4, c % 4
                tall = hidden // 32
                at = [
                    (k, slice((2 * i + side) * tall, (2 * i + side + 1) * tall))
                    for k in range(4)
                    for i in range(2)
                ]
                columns = slice(q * LANES, (q + 2) * LANES)
                own = jnp.concatenate([h_v[2 * k + y, :, lanes] for k, lanes in at], axis=1)
                theirs = jnp.concatenate([r.hn_v[k, :, lanes] for k, lanes in at], axis=1)
                part = dot_cols(own, g_v[:, columns]) + dot_cols(theirs, r.gn_v[:, columns])
            for n, k in enumerate(both):
                first = first_of(kind, k)
                block = part[:, n * LANES : (n + 1) * LANES].astype(BF16)
                first[...] = block.reshape(first.shape)
        elif kind == ATT and c == 2:
            part = dot_cols(o_v[...], dz1_v[...]).astype(BF16)
            tall = inner // 16
            for n in range(4):
                base = base_of(kind, c + n // 2)
                block = part[:, n * LANES : (n + 1) * LANES]
                n = n % 2
                base[:, :, :, n * tall : (n + 1) * tall, :] = block.reshape(
                    base.shape[:3] + (tall, LANES)
                )
        elif kind == ATT:
            if c == 0:
                left = j_v[:, pl.ds(patches, latents), :].reshape(rows, width)
                part = dot_cols(left, dq_v[...])
            else:
                keys = images * (patches + latents)
                at = (c - 4) * LANES
                right = kv_v[:, :, at : at + 2 * LANES].reshape(keys, 2 * LANES)
                part = dot_cols(j_v[...].reshape(keys, width), right)
            for n, k in enumerate(both):
                base = base_of(kind, k)
                block = part[:, n * LANES : (n + 1) * LANES].astype(BF16)
                base[...] = block.reshape(base.shape)
        else:
            lines = r.lines[...]
            for j in range(16):
                own = lines[:, j * 64 : (j + 1) * 64]
                value = jnp.concatenate([own[:40], own[40:]], axis=1)
                r.base_s[j // 4, j // 2 % 2, j % 2] = value

    def first_copy(kind, c, order="xyz"):
        base, first = base_of(kind, c), first_of(kind, c)
        if order == "xyz":
            return remote(kind, c, 0, base.at[:, :, 1 - x], first, at_x)
        return remote(kind, c, 0, base.at[:, 1 - y], first, at_y)

    def second_copy(kind, c, order="xyz"):
        first, second = first_of(kind, c), second_of(kind, c)
        if order == "xyz":
            return remote(kind, c, 1, first.at[:, 1 - y], second, at_y)
        return remote(kind, c, 1, first.at[:, 1 - x], second, at_x)

    def end_copy(kind, c):
        if kind == UP:
            return remote(UP, c, 7, r.end_src.at[c], r.end_u.at[c], at_x)
        return remote(DOWN, c, 7, r.z_d.at[c, z, 1 - x], r.end_d.at[c], at_x)

    def begin(kind, c):
        both = [c] if kind == SMALL else [c, c + 1]
        for k in both:
            old = before(kind, k)
            if kind == UP and 0 <= old < CHUNKS:
                second_copy(UP, old).wait_send()
            if kind == ATT and 0 <= old < CHUNKS:
                first_copy(ATT, old).wait_send()
        compute(kind, c)
        for k in both:
            if paired(kind, k):
                second_copy(kind, k, order_of(kind, k)).start()
            elif kind == DOWN:
                z_start(kind, k)
            else:
                ordered(kind, k, lambda order: first_copy(kind, k, order).start())

    def exchange(k, b, src, dst, where):
        return pltpu.make_async_remote_copy(
            src_ref=src,
            dst_ref=dst,
            send_sem=r.pair_send.at[k, b],
            recv_sem=r.pair_recv.at[k, b],
            device_id=where,
            device_id_type=MESH,
        )

    def span_of(b):
        return pl.ds(pl.multiple_of(b * per, per), per)

    def exchange_f(b):
        return exchange(0, b, f_v.at[span_of(b)], r.fn_v.at[span_of(b)], at_x)

    def exchange_u(b):
        src = sl_v.at[pl.ds(4 * (1 - x), 4), span_of(b)]
        return exchange(1, b, src, r.un_v.at[:, span_of(b)], at_x)

    def exchange_g(b):
        return exchange(2, b, g_v.at[span_of(b)], r.gn_v.at[span_of(b)], at_y)

    def exchange_h(b):
        src = h_v.reshape(4, 2, rows, STEP).at[:, 1 - y, span_of(b)]
        return exchange(3, b, src, r.hn_v.at[:, span_of(b)], at_y)


    def phase_one(wq_v, wo_v, wu_v, wd_v, z_v, q_v, p_v, z1_v, y_v, acc, do_v, mask_v):
        greet()
        loads = [
            load(0, r.wkv, wkv_v),
            load(1, r.wq, wq_v),
            load(2, r.wo, wo_v),
            load(3, r.wu, wu_v),
            load(4, r.wd, wd_v),
        ]
        media_load(0).start()
        loads[0].start()
        for i in range(1, images):
            media_load(i).start()
        for copy in loads[1:]:
            copy.start()
        g_load = load(5, r.cotangent, g_v)

        def start_load(i):
            return load(6 + images, r.start, z_v.at[pl.ds(i * latents, latents)])

        @pl.when(section == 0)
        def _():
            for i in range(images):
                start_load(i).start()

        @pl.when(section == 1)
        def _():
            g_load.start()

        row_head = lax.broadcasted_iota(jnp.int32, (heads * latents, LANES), 0) // latents
        lane_head = lax.broadcasted_iota(jnp.int32, (heads * latents, LANES), 1) // HEAD_DIM
        mask_v[...] = jnp.where(row_head == lane_head, 1.0, 0.0).astype(BF16)
        r.lines[...] = jnp.zeros_like(r.lines)

        loads[0].wait()

        pieces = 4
        tall = patches // pieces
        wide = 2 * inner // pieces

        def media_piece(i, n):
            span = slice(n * tall, (n + 1) * tall)
            hat, _ = normed(j_v[i, span, :].astype(F32))
            low = (hat * r.media_gain[...] + r.media_bias[...]).astype(BF16)
            j_v[i, span, :] = low
            return low

        def media_all():
            media_load(0).wait()
            low = jnp.concatenate([media_piece(0, n) for n in range(pieces)], axis=0)
            for i in range(images):
                later = []
                if i + 1 < images:
                    media_load(i + 1).wait()
                for n in range(pieces):
                    lanes = slice(n * wide, (n + 1) * wide)
                    kv_v[i, :patches, lanes] = dot(low, wkv_v[:, lanes]).astype(BF16)
                    if i + 1 < images:
                        later.append(media_piece(i + 1, n))
                if later:
                    low = jnp.concatenate(later, axis=0)

        media_all()
        for copy in loads[1:]:
            copy.wait()

        @pl.when(section == 0)
        def _():
            load(6 + images, z_v, z_v).wait()

        @pl.when(section == 1)
        def _():
            g_load.wait()
            for i in range(images):
                span = slice(i * latents, (i + 1) * latents)
                live = r.live[i].astype(F32)
                g_v[span, :] = (g_v[span, :].astype(F32) * live).astype(BF16)

        met()
        if fused:

            @pl.when(section == 1)
            def _():
                for b in range(batches):
                    exchange_g(b).start()


        def relay_latents(b):
            span = pl.ds(b * per, per)
            return pltpu.make_async_remote_copy(
                src_ref=y_v.at[span],
                dst_ref=z_v.at[span],
                send_sem=r.send_sem.at[b],
                recv_sem=r.recv_sem.at[b],
                device_id=sibling,
                device_id_type=MESH,
            )

        def relay_grad(b):
            span = pl.ds(b * per, per)
            return pltpu.make_async_remote_copy(
                src_ref=y_v.at[span],
                dst_ref=g_v.at[span],
                send_sem=r.send_sem.at[batches + b],
                recv_sem=r.recv_sem.at[batches + b],
                device_id=sibling,
                device_id_type=MESH,
            )

        def spread(block):
            return jnp.concatenate([block] * heads, axis=0) * mask_v[...]

        def gathered(block):
            lane = lax.broadcasted_iota(jnp.int32, (latents, LANES), 1) // HEAD_DIM
            total = block[0:latents]
            for k in range(1, heads):
                total = jnp.where(lane == k, block[k * latents : (k + 1) * latents], total)
            return total

        def chains(i, local):
            for k in range(TOGETHER):
                at = pl.ds(pl.multiple_of((i + k) * latents, latents), latents)
                here = slice((local + k) * latents, (local + k + 1) * latents)
                for n in range(groups):
                    lanes = slice(n * LANES, (n + 1) * LANES)
                    values = slice(inner + n * LANES, inner + (n + 1) * LANES)
                    yield i + k, (i + k) * groups + n, at, here, lanes, values

        def attend(i):
            todo = list(chains(i, 0))
            scores = [
                dot_rows(kv_v[img, :, lanes], spread(q_v[at, lanes]))
                for img, _, at, _, lanes, _ in todo
            ]
            e = [jnp.exp(s - jnp.max(s, axis=0, keepdims=True)) for s in scores]
            prob = [(v * (1.0 / jnp.sum(v, axis=0, keepdims=True))).astype(BF16) for v in e]
            for (_, slot, *_), p in zip(todo, prob):
                p_v[slot] = p
            mixed = [dot_cols(p, kv_v[img, :, values]) for (img, *_, values), p in zip(todo, prob)]
            for (_, _, at, _, lanes, _), o in zip(todo, mixed):
                o_v[at, lanes] = gathered(o).astype(BF16)

        def attend_back(i, local):
            todo = list(chains(i, local))
            wide = [spread(do_v[here, lanes]) for _, _, _, here, lanes, _ in todo]
            dprob = [dot_rows(kv_v[c[0], :, c[5]], w) for c, w in zip(todo, wide)]
            dv = [dot(p_v[c[1]], w) for c, w in zip(todo, wide)]
            ds = []
            for c, d in zip(todo, dprob):
                p = p_v[c[1]].astype(F32)
                t = p * d
                ds.append((t - p * jnp.sum(t, axis=0, keepdims=True)).astype(BF16))
            query = [spread(q_v[at, lanes]) for _, _, at, _, lanes, _ in todo]
            dq = [dot_cols(d, kv_v[c[0], :, c[4]]) for c, d in zip(todo, ds)]
            dk = [dot(d, q) for d, q in zip(ds, query)]
            for (img, _, at, _, lanes, values), dq_, dk_, dv_ in zip(todo, dq, dk, dv):
                dq_v[at, lanes] = gathered(dq_).astype(BF16) * BF16(HEAD_DIM**-0.5)
                kv_v[img, :, lanes] = dk_.astype(BF16)
                kv_v[img, :, values] = dv_.astype(BF16)

        def forward(b, carry):
            span = pl.ds(pl.multiple_of(b * per, per), per)

            @pl.when(section == 1)
            def _():
                relay_latents(b).wait_recv()

            zed = z_v[span, :].astype(F32)
            hat, _ = normed(zed)
            low = (hat * r.latent_gain[...] + r.latent_bias[...]).astype(BF16)
            j_v[pl.ds(b * GROUP, GROUP), pl.ds(patches, latents), :] = low.reshape(
                GROUP, latents, width
            )
            q_v[span, :] = (dot(low, wq_v[...]) * HEAD_DIM**-0.5).astype(BF16)
            kv_v[pl.ds(b * GROUP, GROUP), pl.ds(patches, latents), :] = (
                dot(low, wkv_v[...]).astype(BF16).reshape(GROUP, latents, 2 * inner)
            )

            for k in range(0, GROUP, TOGETHER):
                attend(b * GROUP + k)
            mixed = zed + dot(o_v[span, :], wo_v[...])
            z1_v[span, :] = mixed
            hat, _ = normed(mixed)
            low = (hat * r.ff_gain[...] + r.ff_bias[...]).astype(BF16)
            f_v[span, :] = low
            if fused:
                exchange_f(b).start()
            u = dot(low, wu_v[:, 0:STEP])
            for c in range(chunks):
                lanes = slice(c * STEP, (c + 1) * STEP)
                later = None
                if c + 1 < chunks:
                    later = dot(low, wu_v[:, (c + 1) * STEP : (c + 2) * STEP])
                h, slope = gelu_and_slope(u)
                h = h.astype(BF16)
                h_v[c, span, :] = h
                sl_v[c, span, :] = slope.astype(BF16)
                part = dot(h, wd_v[lanes, :])
                acc[...] = part + (mixed if c == 0 else acc[...])
                u = later
            y_v[span, :] = acc[...].astype(BF16)

            @pl.when(section == 0)
            def _():
                relay_latents(b).start()

            if fused:
                @pl.when((section == 1) | (b + 1 < batches))
                def _():
                    exchange_h(b).start()

            return carry

        lax.fori_loop(0, batches, forward, 0)
        y_store = store(0, y_v, r.y_out)
        y_store.start()

        def backward_ff(b, carry):
            span = pl.ds(pl.multiple_of(b * per, per), per)

            @pl.when(section == 0)
            def _():
                if fused:

                    @pl.when(b == 0)
                    def _():
                        pl.semaphore_wait(r.go, 1)
                        exchange_h(batches - 1).start()

                relay_grad(b).wait_recv()
                if fused:
                    exchange_g(b).start()

            g = g_v[span, :]

            def chunk(n):
                return lax.rem(n + chunks // 2 * (1 - x), chunks)

            def part_of(n):
                return pl.ds(pl.multiple_of(chunk(n) * STEP, STEP), STEP)

            dh = dot_rows(g, wd_v[part_of(0), :])
            for n in range(chunks):
                later = None
                if n + 1 < chunks:
                    later = dot_rows(g, wd_v[part_of(n + 1), :])
                du = (dh * sl_v[chunk(n), span, :].astype(F32)).astype(BF16)
                sl_v[chunk(n), span, :] = du
                part = dot_rows(du, wu_v[:, part_of(n)])
                acc[...] = part if n == 0 else acc[...] + part
                dh = later
                if fused and n + 1 == chunks // 2:
                    exchange_u(b).start()
            if fused:
                @pl.when((section == 1) & (b == 0))
                def _():
                    signal(r.go, sibling)

            df = acc[...]
            hat, factor = normed(z1_v[span, :])
            r.lines[4:5, :] += jnp.sum(df * hat, axis=0, keepdims=True)
            r.lines[5:6, :] += jnp.sum(df, axis=0, keepdims=True)
            dz1 = g.astype(F32) + norm_back(df, hat, factor, r.ff_gain[...])
            z1_v[span, :] = dz1
            dz1_v[span, :] = dz1.astype(BF16)
            return carry

        def backward_attention(b, carry):
            span = pl.ds(pl.multiple_of(b * per, per), per)
            do_v[...] = dot_rows(dz1_v[span, :], wo_v[...]).astype(BF16)

            for k in range(0, GROUP, TOGETHER):
                attend_back(b * GROUP + k, k)
            tail = kv_v[pl.ds(b * GROUP, GROUP), pl.ds(patches, latents), :].reshape(per, 2 * inner)
            dn = dot_rows(dq_v[span, :], wq_v[...]) + dot_rows(tail, wkv_v[...])
            hat, factor = normed(z_v[span, :].astype(F32))
            r.lines[2:3, :] += jnp.sum(dn * hat, axis=0, keepdims=True)
            r.lines[3:4, :] += jnp.sum(dn, axis=0, keepdims=True)
            dz = z1_v[span, :] + norm_back(dn, hat, factor, r.latent_gain[...])
            y_v[span, :] = dz.astype(BF16)

            @pl.when(section == 1)
            def _():
                relay_grad(b).start()

            @pl.when(section == 0)
            def _():
                total = dz[0:latents]
                for k in range(1, GROUP):
                    total = total + dz[k * latents : (k + 1) * latents]
                r.lines[8 : 8 + latents, :] += total

            return carry

        y_store.wait()

        @pl.when(section == 0)
        def _():
            for b in range(batches):
                relay_latents(b).wait_send()

        def backward(b, carry):
            return backward_attention(b, backward_ff(b, carry))

        lax.fori_loop(0, batches, backward, 0)

        @pl.when(section == 1)
        def _():
            for b in range(batches):
                relay_grad(b).wait_send()

    pl.run_scoped(
        phase_one,
        pltpu.VMEM(r.wq.shape, BF16),
        pltpu.VMEM(r.wo.shape, BF16),
        pltpu.VMEM(r.wu.shape, BF16),
        pltpu.VMEM(r.wd.shape, BF16),
        pltpu.VMEM((rows, width), BF16),
        pltpu.VMEM((rows, inner), BF16),
        pltpu.VMEM((images * groups, patches + latents, heads * latents), BF16),
        pltpu.VMEM((rows, width), F32),
        pltpu.VMEM((rows, width), BF16),
        pltpu.VMEM((per, width), F32),
        pltpu.VMEM((per, inner), BF16),
        pltpu.VMEM((heads * latents, LANES), BF16),
    )

    if not fused:
        copies = [
            store(k + 1, src, dst)
            for k, (src, dst) in enumerate(
                [
                    (j_v, r.j_out),
                    (kv_v, r.kv_out),
                    (o_v, r.o_out),
                    (f_v, r.f_out),
                    (h_v, r.h_out),
                    (sl_v, r.du_out),
                    (dz1_v, r.dz1_out),
                    (dq_v, r.dq_out),
                    (g_v, r.g_out),
                ]
            )
        ]
        for copy in copies:
            copy.start()
        for copy in copies:
            copy.wait()
        r.lines_out[...] = r.lines[...]
        return


    def z_base(kind, c):
        return first_of(kind, c) if order_of(kind, c) == "zx" else second_of(kind, c)

    def up_copy(kind, c, d, src):
        return remote(kind, c, 2 + d, src, z_of(kind, c).at[d], at_up)

    def down_copy(kind, c, d, src, last):
        place = 4 if last else d
        return remote(kind, c, 2 + place, src, z_of(kind, c).at[place], at_down)

    def add_into(dst, src):
        lead = dst.shape[:-2]
        if not lead:
            dst[...] = halves(dst[...], src[...])
            return
        total = 1
        for size in lead:
            total *= size

        def step(k, carry):
            at = []
            for size in reversed(lead):
                at.append(lax.rem(k, size))
                k = k // size
            at = tuple(reversed(at))
            dst[at] = halves(dst[at], src[at])
            return carry

        lax.fori_loop(0, total, step, 0)

    def send_own(kind, c, d, up):
        src = z_base(kind, c).at[d]
        if up:
            up_copy(kind, c, d, src).start()
        else:
            down_copy(kind, c, d, src, d == 2).start()

    def pass_on(kind, c, d, up, last=False):
        zb = z_of(kind, c)
        up_copy(kind, c, d, zb.at[d]).wait_recv()
        add_into(zb.at[d], z_base(kind, c).at[d])
        if up:
            up_copy(kind, c, d, zb.at[d]).start()
        else:
            down_copy(kind, c, d, zb.at[d], last).start()

    def z_start(kind, c):
        zb = z_of(kind, c)

        @pl.when(z == 0)
        def _():
            zb[0] = jnp.zeros(zb.shape[1:], zb.dtype)
            send_own(kind, c, 3, True)

        @pl.when(z == 3)
        def _():
            zb[4] = jnp.zeros(zb.shape[1:], zb.dtype)
            send_own(kind, c, 0, False)

    def z_near(kind, c):
        @pl.when(z == 0)
        def _():
            send_own(kind, c, 2, True)

        @pl.when(z == 1)
        def _():
            pass_on(kind, c, 3, True)

        @pl.when(z == 2)
        def _():
            pass_on(kind, c, 0, False)

        @pl.when(z == 3)
        def _():
            send_own(kind, c, 1, False)

    def z_far(kind, c):
        @pl.when(z == 0)
        def _():
            send_own(kind, c, 1, True)

        @pl.when(z == 1)
        def _():
            pass_on(kind, c, 0, False, True)
            pass_on(kind, c, 2, True)

        @pl.when(z == 2)
        def _():
            pass_on(kind, c, 3, True)
            pass_on(kind, c, 1, False, True)

        @pl.when(z == 3)
        def _():
            send_own(kind, c, 2, False)

    def z_arrive(kind, c):
        zb = z_of(kind, c)

        @pl.when(z > 0)
        def _():
            remote(kind, c, 2 + z, zb.at[z], zb.at[z], at_up).wait_recv()

        @pl.when(z < 3)
        def _():
            remote(kind, c, 6, zb.at[4], zb.at[4], at_down).wait_recv()

    def finish(kind, c, total):
        def put(k, rows_at, lanes_at, value):
            held, out = results()[k]
            held[rows_at, lanes_at] = value
            out_copy(held.at[rows_at, lanes_at], out.at[rows_at, lanes_at], k).start()

        tall = total.shape[0]
        if kind == DOWN:
            rows_at, lanes_at = down_at(c)
            put(1, rows_at, lanes_at, total)
        elif kind == ATT and c < 2:
            put(2, slice(0, tall), slice(c * LANES, (c + 1) * LANES), total)
        elif kind == ATT and c < 4:
            tall = tall // 2
            for n in range(2):
                at = ((c - 2) * 2 + n) * LANES
                value = total[n * tall : (n + 1) * tall]
                put(3, slice(0, tall), slice(at, at + LANES), value)
        elif kind == ATT:
            at = (c - 4) * LANES
            put(4, slice(0, tall), slice(at, at + LANES), total)
        else:
            r.small_out[...] = total

            @pl.when(section == 0)
            def _():
                relay_start().start()
                own_start().start()

    def relay_start():
        last = 2 * batches + images
        return pltpu.make_async_remote_copy(
            src_ref=r.small_out,
            dst_ref=r.start_out,
            send_sem=r.send_sem.at[last],
            recv_sem=r.recv_sem.at[last],
            device_id=sibling,
            device_id_type=MESH,
        )

    def own_start():
        return store(9, r.small_out, r.start_out)

    def results():
        return (
            (r.up_out, r.up_out),
            (r.down_v, r.down_out),
            (r.query_v, r.query_out),
            (r.out_v, r.out_out),
            (r.keyval_v, r.keyval_out),
        )

    def out_copy(src, dst, k):
        return pltpu.make_async_copy(src, dst, r.out_sem.at[k])

    def down_at(c):
        tall = hidden // 32
        return slice(c // 4 * tall, (c // 4 + 1) * tall), slice(c % 4 * LANES, (c % 4 + 1) * LANES)

    def put_up(c, n, half, total):
        held = r.up_v.at[n, :, pl.ds(c * LANES, LANES)]
        held[...] = total
        at = pl.multiple_of(half * (hidden // 2) + c * LANES, LANES)
        out_copy(held, r.up_out.at[:, pl.ds(at, LANES)], 0).start()

    def advance(kind, c, step):
        zb = z_of(kind, c)
        if kind == DOWN and c < DOWN_Z:
            base = first_of(kind, c)
            if step == 1:
                z_near(kind, c)
            elif step == 2:
                z_far(kind, c)
            elif step == 3:
                z_arrive(kind, c)
                total = base[z, 1 - x].astype(F32) + zb[z, 1 - x].astype(F32)
                zb[z, 1 - x] = (total + zb[4, 1 - x].astype(F32)).astype(BF16)
                end_copy(kind, c).start()
                total = base[z, x].astype(F32) + zb[z, x].astype(F32)
                r.down_v[down_at(c)] = total + zb[4, x].astype(F32)
            elif step == 4:
                end_copy(kind, c).wait_recv()
                finish(kind, c, r.down_v[down_at(c)] + r.end_d[c].astype(F32))
            return
        first, second = first_of(kind, c), second_of(kind, c)

        def add_first(order):
            base = base_of(kind, c)
            add_into(first, base.at[:, :, x] if order == "xyz" else base.at[:, y])
            second_copy(kind, c, order).start()

        def add_second(order):
            add_into(second, first.at[:, y] if order == "xyz" else first.at[:, x])

        if step == 1:
            first_copy(kind, c).wait_recv()
            ordered(kind, c, add_first)
        elif step == 2:
            second_copy(kind, c).wait_recv()
            ordered(kind, c, add_second)
            z_start(kind, c)
        elif step == 3:
            z_near(kind, c)
        elif step == 4:
            z_far(kind, c)
        elif step == 5 and kind == UP:
            z_arrive(kind, c)
            total = second[z, 1 - x].astype(F32) + zb[z, 1 - x].astype(F32)
            r.end_src[c] = (total + zb[4, 1 - x].astype(F32)).astype(BF16)
            end_copy(kind, c).start()
            total = second[z, x].astype(F32) + zb[z, x].astype(F32)
            put_up(c, 0, x, total + zb[4, x].astype(F32))
        elif step == 5:
            z_arrive(kind, c)
            total = second[z].astype(F32) + zb[z].astype(F32)
            finish(kind, c, total + zb[4].astype(F32))
        elif step == 6 and kind == UP:
            end_copy(kind, c).wait_recv()
            put_up(c, 1, 1 - x, r.end_u[c].astype(F32))

    def sends_done():
        for kind, c in BLOCKS:
            taken = 0 <= 2 * c - before(kind, c) < CHUNKS
            if kind == SMALL or (kind == ATT and not taken):
                first_copy(kind, c).wait_send()
            if not (kind == DOWN and c < DOWN_Z) and not (kind == UP and taken):
                second_copy(kind, c).wait_send()
            if kind == UP or (kind == DOWN and c < DOWN_Z):
                end_copy(kind, c).wait_send()
        for kind, along in (
            (UP, r.z_u),
            (DOWN, r.z_d),
            (DOWN, r.z_d_late),
            (ATT, r.z_a),
            (SMALL, r.z_s),
        ):
            along = along.at[0:3] if kind == SMALL else along.at[:, 0:3]
            remote(kind, 0, 2, along, along, at_x).wait_send()
        for b in range(batches):
            for copy in (exchange_f(b), exchange_u(b), exchange_g(b), exchange_h(b)):
                copy.wait_send()

    def phase_two(*buffers):
        names_two = ["first_u", "second_u", "z_u", "end_src", "end_u", "first_d"]
        names_two += ["second_d", "z_d", "z_d_late", "end_d"]
        names_two += ["base_a", "first_a", "second_a", "z_a"]
        names_two += ["base_s", "first_s", "second_s", "z_s", "media_v", "mine_v", "other_v"]
        names_two += ["up_v", "down_v", "keyval_v", "query_v", "out_v"]
        r.__dict__.update(zip(names_two, buffers, strict=True))
        media_v, mine_v, other_v = r.media_v, r.mine_v, r.other_v

        signal(r.ready.at[0], at_x)
        signal(r.ready.at[1], at_y)

        @pl.when(z < 3)
        def _():
            signal(r.ready.at[2], at_up)

        @pl.when(z > 0)
        def _():
            signal(r.ready.at[3], at_down)

        def urgency(entry):
            step, kind, c = entry
            return step == final(kind, c), final(kind, c) - step, kind, c

        def image_load(i):
            return load(6 + i, r.media.at[i], media_v.at[i % 2])

        def mine_store(i):
            return store(1 + i, mine_v, r.mine_out.at[i])

        def relay_media(i):
            return pltpu.make_async_remote_copy(
                src_ref=other_v.at[i % 2],
                dst_ref=r.theirs_out.at[i],
                send_sem=r.send_sem.at[2 * batches + i],
                recv_sem=r.recv_sem.at[2 * batches + i],
                device_id=sibling,
                device_id_type=MESH,
            )

        def media_grad(i):
            half = width // 2
            image_load(i).wait()
            dj = dot_rows(kv_v[i, pl.ds(0, patches), :], wkv_v[...])
            hat, factor = normed(media_v[i % 2].astype(F32))
            r.lines[0:1, :] += jnp.sum(dj * hat, axis=0, keepdims=True)
            r.lines[1:2, :] += jnp.sum(dj, axis=0, keepdims=True)
            grad = norm_back(dj, hat, factor, r.media_gain[...])
            if i >= 1:
                mine_store(i - 1).wait()
            if i >= 2:
                relay_media(i - 2).wait_send()

            @pl.when(section == 0)
            def _():
                mine_v[...] = grad[:, :half]
                other_v[i % 2] = grad[:, half:].astype(BF16)

            @pl.when(section == 1)
            def _():
                mine_v[...] = grad[:, half:]
                other_v[i % 2] = grad[:, :half].astype(BF16)

            mine_store(i).start()
            relay_media(i).start()
            if i + 2 < images:
                image_load(i + 2).start()

        image_load(0).start()
        image_load(1).start()
        pl.semaphore_wait(r.ready.at[0], 1)
        pl.semaphore_wait(r.ready.at[1], 1)

        @pl.when(z > 0)
        def _():
            pl.semaphore_wait(r.ready.at[2], 1)

        @pl.when(z < 3)
        def _():
            pl.semaphore_wait(r.ready.at[3], 1)

        slots = {(SMALL, 0): SMALL_SLOT}
        for kind, at in ((DOWN, DOWN_SLOTS), (ATT, ATT_SLOTS), (UP, UP_SLOTS)):
            slots.update({(kind, c): slot for c, slot in enumerate(at)})
        last = max(slots.values()) + 7
        for b in range(batches):
            exchange_g(b).wait_recv()
            exchange_h(b).wait_recv()

        def final(kind, c):
            return 6 if kind == UP else 4 if kind == DOWN and c < DOWN_Z else 5

        def slot_of(kind, c, step):
            return slots[kind, c] + step - paired(kind, c)

        for slot in range(last):
            for (kind, c), at in slots.items():
                if at == slot and c % 2 == 0:
                    if kind == UP and c == 0:
                        for b in range(batches):
                            exchange_f(b).wait_recv()
                            exchange_u(b).wait_recv()
                    begin(kind, c)
            live = []
            for kind, c in slots:
                steps = range(1 + paired(kind, c), final(kind, c) + 1)
                live += [(n, kind, c) for n in steps if slot_of(kind, c, n) == slot]
            for step, kind, c in sorted(live, key=urgency):
                advance(kind, c, step)
            for i in range(images):
                if MEDIA_SLOTS[i] == slot:
                    media_grad(i)

        sends_done()
        mine_store(images - 1).wait()
        for i in range(images - 2, images):
            relay_media(i).wait_send()
        for i in range(images):
            relay_media(i).wait_recv()
        for k, (held, out) in enumerate(results()):
            out_copy(held, out, k).wait()

        @pl.when(section == 0)
        def _():
            relay_start().wait_send()
            own_start().wait()

        @pl.when(section == 1)
        def _():
            relay_start().wait_recv()

    tile_u, tile_d = (width // 16, LANES), (hidden // 32, LANES)
    tile_a, tile_s = (width // 16, LANES), (40, 128)
    pl.run_scoped(
        phase_two,
        pltpu.VMEM((RING, 4, 2, 2) + tile_u, BF16),
        pltpu.VMEM((CHUNKS, 4, 2) + tile_u, BF16),
        pltpu.VMEM((CHUNKS, 5, 2) + tile_u, BF16),
        pltpu.VMEM((CHUNKS,) + tile_u, BF16),
        pltpu.VMEM((CHUNKS,) + tile_u, BF16),
        pltpu.VMEM((CHUNKS, 4, 2) + tile_d, BF16),
        pltpu.VMEM((CHUNKS - DOWN_Z, 4) + tile_d, BF16),
        pltpu.VMEM((DOWN_Z, 5, 2) + tile_d, BF16),
        pltpu.VMEM((CHUNKS - DOWN_Z, 5) + tile_d, BF16),
        pltpu.VMEM((DOWN_Z,) + tile_d, BF16),
        pltpu.VMEM((RING, 4, 2, 2) + tile_a, BF16),
        pltpu.VMEM((CHUNKS, 4, 2) + tile_a, BF16),
        pltpu.VMEM((CHUNKS, 4) + tile_a, BF16),
        pltpu.VMEM((CHUNKS, 5) + tile_a, BF16),
        pltpu.VMEM((4, 2, 2) + tile_s, F32),
        pltpu.VMEM((4, 2) + tile_s, F32),
        pltpu.VMEM((4,) + tile_s, F32),
        pltpu.VMEM((5,) + tile_s, F32),
        pltpu.VMEM((2, patches, width), BF16),
        pltpu.VMEM((patches, width // 2), F32),
        pltpu.VMEM((2, patches, width // 2), BF16),
        pltpu.VMEM((2, width // 16, hidden // 2), F32),
        pltpu.VMEM((hidden // 16, width), F32),
        pltpu.VMEM((width // 16, 2 * inner), F32),
        pltpu.VMEM((width // 16, inner), F32),
        pltpu.VMEM((inner // 16, width), F32),
    )


def layers(fused, start, media, cotangent, live, lines, wq, wkv, wo, wu, wd):
    images, patches, width = media.shape
    latents = start.shape[0]
    inner = wq.shape[1]
    hidden = wu.shape[1]
    rows = images * latents
    batches = images // GROUP
    dims = (images, latents, patches, inner, hidden, width)
    keys = patches + latents
    any_spec = pl.BlockSpec(memory_space=pl.ANY)
    vmem_spec = pl.BlockSpec(memory_space=pltpu.VMEM)
    smem_spec = pl.BlockSpec(memory_space=pltpu.SMEM)

    def low(*shape):
        return jax.ShapeDtypeStruct(shape, BF16)

    def full(*shape):
        return jax.ShapeDtypeStruct(shape, F32)

    ins = [
        ("start", start, any_spec),
        ("media", media, any_spec),
        ("cotangent", cotangent, any_spec),
        ("live", live, smem_spec),
    ]
    line_names = ["media_gain", "media_bias", "latent_gain", "latent_bias", "ff_gain", "ff_bias"]
    ins += [(n, a, vmem_spec) for n, a in zip(line_names, lines, strict=True)]
    ins += [(n, a, any_spec) for n, a in zip(("wq", "wkv", "wo", "wu", "wd"), (wq, wkv, wo, wu, wd))]
    outs = [("y_out", low(rows, width), any_spec)]
    if fused:
        outs += [
            ("mine_out", full(images, patches, width // 2), any_spec),
            ("theirs_out", low(images, patches, width // 2), any_spec),
            ("up_out", full(width // 16, hidden), any_spec),
            ("down_out", full(hidden // 16, width), any_spec),
            ("keyval_out", full(width // 16, 2 * inner), any_spec),
            ("query_out", full(width // 16, inner), any_spec),
            ("out_out", full(inner // 16, width), any_spec),
            ("start_out", full(40, 128), any_spec),
            ("small_out", full(40, 128), vmem_spec),
        ]
    else:
        outs += [
            ("j_out", low(images, keys, width), any_spec),
            ("kv_out", low(images, keys, 2 * inner), any_spec),
            ("o_out", low(rows, inner), any_spec),
            ("f_out", low(rows, width), any_spec),
            ("h_out", low(hidden // STEP, rows, STEP), any_spec),
            ("du_out", low(hidden // STEP, rows, STEP), any_spec),
            ("dz1_out", low(rows, width), any_spec),
            ("dq_out", low(rows, inner), any_spec),
            ("g_out", low(rows, width), any_spec),
            ("lines_out", full(80, width), vmem_spec),
        ]
    scratch = [
        ("wkv_v", pltpu.VMEM(wkv.shape, BF16)),
        ("j_v", pltpu.VMEM((images, keys, width), BF16)),
        ("kv_v", pltpu.VMEM((images, keys, 2 * inner), BF16)),
        ("o_v", pltpu.VMEM((rows, inner), BF16)),
        ("f_v", pltpu.VMEM((rows, width), BF16)),
        ("h_v", pltpu.VMEM((hidden // STEP, rows, STEP), BF16)),
        ("sl_v", pltpu.VMEM((hidden // STEP, rows, STEP), BF16)),
        ("g_v", pltpu.VMEM((rows, width), BF16)),
        ("dz1_v", pltpu.VMEM((rows, width), BF16)),
        ("dq_v", pltpu.VMEM((rows, inner), BF16)),
        ("lines", pltpu.VMEM((80, width), F32)),
        ("load_sem", pltpu.SemaphoreType.DMA((7 + images,))),
        ("store_sem", pltpu.SemaphoreType.DMA((10,))),
        ("send_sem", pltpu.SemaphoreType.DMA((2 * batches + images + 1,))),
        ("recv_sem", pltpu.SemaphoreType.DMA((2 * batches + images + 1,))),
    ]
    if fused:
        scratch += [
            ("hn_v", pltpu.VMEM((4, rows, STEP), BF16)),
            ("gn_v", pltpu.VMEM((rows, width), BF16)),
            ("fn_v", pltpu.VMEM((rows, width), BF16)),
            ("un_v", pltpu.VMEM((4, rows, STEP), BF16)),
            ("pair_send", pltpu.SemaphoreType.DMA((4, batches))),
            ("pair_recv", pltpu.SemaphoreType.DMA((4, batches))),
            ("rs_send", pltpu.SemaphoreType.DMA((2 * len(BLOCKS) + 5,))),
            ("rs_recv", pltpu.SemaphoreType.DMA((len(BLOCKS), 8))),
            ("out_sem", pltpu.SemaphoreType.DMA((5,))),
            ("go", pltpu.SemaphoreType.REGULAR),
            ("ready", pltpu.SemaphoreType.REGULAR((4,))),
        ]
    names = [n for n, *_ in ins] + [n for n, *_ in outs] + [n for n, _ in scratch]
    results = pl.pallas_call(
        functools.partial(layer_kernel, dims, fused, names),
        out_shape=[s for _, s, _ in outs],
        in_specs=[s for _, _, s in ins],
        out_specs=[s for _, _, s in outs],
        scratch_shapes=[s for _, s in scratch],
        compiler_params=pltpu.CompilerParams(
            collective_id=1, has_side_effects=True, vmem_limit_bytes=VMEM_LIMIT
        ),
        name="layers",
    )(*[a for _, a, _ in ins])
    return Refs([n for n, *_ in outs], results)


def media_kernel(dims, dkv, media, wkv, gain, mine, other, sums):
    patches, half = dims
    section = lax.axis_index("section")

    @pl.when(pl.program_id(0) == 0)
    def _():
        sums[...] = jnp.zeros_like(sums)

    dj = dot_rows(dkv[0], wkv[...])
    hat, factor = normed(media[0].astype(F32))
    sums[0:1, :] += jnp.sum(dj * hat, axis=0, keepdims=True)
    sums[1:2, :] += jnp.sum(dj, axis=0, keepdims=True)
    grad = norm_back(dj, hat, factor, gain[...])

    @pl.when(section == 0)
    def _():
        mine[0] = grad[:, :half]
        other[0] = grad[:, half:].astype(BF16)

    @pl.when(section == 1)
    def _():
        mine[0] = grad[:, half:]
        other[0] = grad[:, :half].astype(BF16)


def media_grads(dkv, media, wkv, gain):
    images, patches, width = media.shape
    half = width // 2
    return pl.pallas_call(
        functools.partial(media_kernel, (patches, half)),
        grid=(images,),
        out_shape=[
            jax.ShapeDtypeStruct((images, patches, half), F32),
            jax.ShapeDtypeStruct((images, patches, half), BF16),
            jax.ShapeDtypeStruct((8, width), F32),
        ],
        in_specs=[
            pl.BlockSpec((1, patches, dkv.shape[2]), lambda i: (i, 0, 0)),
            pl.BlockSpec((1, patches, width), lambda i: (i, 0, 0)),
            pl.BlockSpec(wkv.shape, lambda i: (0, 0)),
            pl.BlockSpec((1, width), lambda i: (0, 0)),
        ],
        out_specs=[
            pl.BlockSpec((1, patches, half), lambda i: (i, 0, 0)),
            pl.BlockSpec((1, patches, half), lambda i: (i, 0, 0)),
            pl.BlockSpec((8, width), lambda i: (0, 0)),
        ],
        compiler_params=pltpu.CompilerParams(vmem_limit_bytes=48 * 1024 * 1024),
        name="media_grads",
    )(dkv, media, wkv, gain)


def hand_over_kernel(latents, mine, theirs, small, start, *refs):
    count = (len(refs) - 8) // 2
    sources, media_out, start_out = refs[:count], refs[count], refs[count + 1]
    lines, targets = refs[count + 2 : count + 8], refs[count + 8 :]
    section = lax.axis_index("section")

    @pl.when(pl.program_id(0) == 0)
    def _():
        for k, line in enumerate(lines):
            line[...] = small[k : k + 1, :64]

        @pl.when(section == 0)
        def _():
            start_out[...] = start[8 : 8 + latents // 2, :64]

        @pl.when(section == 1)
        def _():
            start_out[...] = start[: latents // 2, 64:]

    media_out[...] = mine[...] + theirs[...].astype(F32)
    for source, target in zip(sources, targets):
        target[...] = source[...]


def hand_over(latents, mine, theirs, small, start, arrays):
    images, patches, half = mine.shape
    steps = 4
    media_spec = pl.BlockSpec((images // steps, patches, half), lambda i: (i, 0, 0))

    def whole(shape):
        return pl.BlockSpec(shape, lambda i: (0, 0))

    line, start_shape = (1, 64), (latents // 2, 64)
    parts = [
        pl.BlockSpec((a.shape[0] // steps, a.shape[1]), lambda i: (i, 0))
        if a.shape[0] % (8 * steps) == 0
        else whole(a.shape)
        for a in arrays
    ]
    return pl.pallas_call(
        functools.partial(hand_over_kernel, latents),
        grid=(steps,),
        out_shape=[jax.ShapeDtypeStruct(mine.shape, F32), jax.ShapeDtypeStruct(start_shape, F32)]
        + [jax.ShapeDtypeStruct(line, F32)] * 6
        + [jax.ShapeDtypeStruct(a.shape, a.dtype) for a in arrays],
        in_specs=[media_spec, media_spec, whole(small.shape), whole(start.shape)] + parts,
        out_specs=[media_spec, whole(start_shape)] + [whole(line)] * 6 + parts,
        compiler_params=pltpu.CompilerParams(vmem_limit_bytes=VMEM_LIMIT),
        name="hand_over",
    )(mine, theirs, small, start, *arrays)


def weight_grad(left, right):
    left = left.reshape(-1, left.shape[-1])
    right = right.reshape(-1, right.shape[-1])
    return dot_cols(left, right).astype(BF16)


def swap_sections(value):
    return lax.ppermute(value, "section", [(0, 1), (1, 0)])


def shards(
    media,
    image_live,
    start_latents,
    latent_cotangent,
    media_gain,
    media_bias,
    latent_gain,
    latent_bias,
    w_query,
    w_kv,
    w_out,
    ff_gain,
    ff_bias,
    w_up,
    w_down,
):
    images, patches, width = media.shape
    latents = start_latents.shape[0]
    peers = lax.axis_size("dp")
    rows = images * latents
    fused = peers == 16
    wkv = w_kv[0]
    k = layers(
        fused,
        start_latents,
        media,
        latent_cotangent.reshape(rows, width),
        image_live,
        (media_gain, media_bias, latent_gain, latent_bias, ff_gain, ff_bias),
        w_query[0],
        wkv,
        w_out[0],
        w_up[0],
        w_down[0],
    )
    if fused:
        media_grad, start_grad, *rest = hand_over(
            latents,
            k.mine_out,
            k.theirs_out,
            k.small_out,
            k.start_out,
            [k.y_out, k.query_out, k.keyval_out, k.out_out, k.up_out, k.down_out],
        )
        lines = rest[:6]
        y_low, query, kv, out, up, down = rest[6:]
    else:
        mine, other, media_sums = media_grads(k.kv_out, media, wkv, media_gain)
        theirs = swap_sections(other)
        up, down, kv, query, out = (
            lax.psum_scatter(a, "dp", scatter_dimension=0, tiled=True).astype(F32)
            for a in (
                weight_grad(k.f_out, k.du_out.swapaxes(0, 1).reshape(rows, -1)),
                weight_grad(k.h_out.swapaxes(0, 1).reshape(rows, -1), k.g_out),
                weight_grad(k.j_out, k.kv_out),
                weight_grad(k.j_out[:, patches:], k.dq_out),
                weight_grad(k.o_out, k.dz1_out),
            )
        )
        y_low = k.y_out
        lines = jnp.concatenate([media_sums[:2], k.lines_out[2:6]], axis=0)
        lines = lax.psum_scatter(lines, "dp", scatter_dimension=1, tiled=True)
        lines = jnp.split(lines, 6, axis=0)
        start_part = lax.psum_scatter(
            k.lines_out[8 : 8 + latents], "dp", scatter_dimension=1, tiled=True
        )
        half = latents // 2
        far = swap_sections(start_part[half:])
        start_grad = jnp.where(lax.axis_index("section") == 0, start_part[:half], far)
        media_grad = mine + theirs.astype(F32)
    return (
        y_low.reshape(1, images, latents, width),
        media_grad,
        start_grad,
        *lines[:4],
        query[None],
        kv[None],
        out[None],
        *lines[4:],
        up[None],
        down[None],
    )


def solution(mesh):
    row = P("section", None)
    mat = P("section", None, None)
    in_specs = (
        P("dp", None, None), P("dp"), P(), P("dp", None, None),
        row, row, row, row, mat, mat, mat, row, row, mat, mat,
    )
    line = P("section", "dp")
    block = P("section", "dp", None)
    out_specs = (
        P("section", "dp", None, None), P("dp", None, "section"), line,
        line, line, line, line, block, block, block, line, line, block, block,
    )
    return jax.shard_map(shards, mesh=mesh, in_specs=in_specs, out_specs=out_specs, check_vma=False)
```

```python
import functools

import jax
import jax.numpy as jnp
from jax import lax
from jax.experimental import pallas as pl
from jax.experimental.pallas import tpu as pltpu
from jax.sharding import PartitionSpec as P

MESH = pl.DeviceIdType.MESH
F32 = jnp.float32
BF16 = jnp.bfloat16
HEAD_DIM = 64
LANES = 256
GROUP = 4
TOGETHER = 4
STEP = 512
VMEM_LIMIT = 63 * 1024 * 1024


def dot(left, right):
    return jnp.dot(left, right, preferred_element_type=F32)


def dot_rows(left, right):
    return lax.dot_general(left, right, (((1,), (1,)), ((), ())), preferred_element_type=F32)


def dot_cols(left, right):
    return lax.dot_general(left, right, (((0,), (0,)), ((), ())), preferred_element_type=F32)


def normed(value):
    centred = value - jnp.mean(value, axis=-1, keepdims=True)
    factor = lax.rsqrt(jnp.mean(centred * centred, axis=-1, keepdims=True) + 1e-05)
    return centred * factor, factor


def norm_back(upstream, hat, factor, gain):
    scaled = upstream * gain
    return factor * (
        scaled
        - jnp.mean(scaled, axis=-1, keepdims=True)
        - hat * jnp.mean(scaled * hat, axis=-1, keepdims=True)
    )


def gelu_and_slope(u):
    e = jnp.exp2((u * u) * (-0.5 * 1.4426950408889634))
    t = pl.reciprocal(1.0 + jnp.abs(u) * (0.3275911 * 0.7071067811865476), approx=True)
    tail = t * (
        0.127414796 + t * (-0.142248368 + t * (0.7107068705 + t * (-0.7265760135 + t * 0.5307027145)))
    )
    tail = tail * e
    phi = jnp.where(u >= 0.0, 1.0 - tail, tail)
    return u * phi, phi + (u * e) * 0.3989422804014327


def halves(a, b):
    return (a.astype(F32) + b.astype(F32)).astype(a.dtype)


class Refs:
    def __init__(self, names, refs):
        self.__dict__.update(zip(names, refs, strict=True))


UP, DOWN, ATT, SMALL = 0, 1, 2, 3
CHUNKS = 8
RING = 4
DOWN_Z = 4
DOWN_SLOTS = (0, 0, 1, 1, 3, 3, 4, 4)
UP_SLOTS = (2, 2, 3, 3, 4, 4, 5, 5)
ATT_SLOTS = (5, 5, 6, 6, 3, 3, 4, 4)
MEDIA_SLOTS = (0, 0, 1, 1, 2, 3, 4, 4)
SMALL_SLOT = 5
BLOCKS = [(kind, c) for kind in (UP, DOWN, ATT) for c in range(CHUNKS)] + [(SMALL, 0)]


def layer_kernel(dims, fused, names, *all_refs):
    images, latents, patches, inner, hidden, width = dims
    r = Refs(names, all_refs)
    rows = images * latents
    per = GROUP * latents
    batches = images // GROUP
    groups = inner // LANES
    heads = LANES // HEAD_DIM
    chunks = hidden // STEP
    section = lax.axis_index("section")
    dp = lax.axis_index("dp")
    sibling = (1 - section, dp)
    x = lax.rem(dp, 2)
    y = lax.rem(dp // 2, 2)
    z = dp // 4
    at_x = (section, dp + 1 - 2 * x)
    at_y = (section, dp + 2 - 4 * y)
    at_up = (section, dp + 4)
    at_down = (section, dp - 4)
    j_v, kv_v, o_v, f_v, h_v, sl_v = r.j_v, r.kv_v, r.o_v, r.f_v, r.h_v, r.sl_v
    g_v, dz1_v, dq_v, wkv_v = r.g_v, r.dz1_v, r.dq_v, r.wkv_v

    def signal(sem, where):
        pl.semaphore_signal(sem, inc=1, device_id=where, device_id_type=MESH)

    def load(k, src, dst):
        return pltpu.make_async_copy(src, dst, r.load_sem.at[k])

    def store(k, src, dst):
        return pltpu.make_async_copy(src, dst, r.store_sem.at[k])

    def media_load(i):
        return load(6 + i, r.media.at[i], j_v.at[i, pl.ds(0, patches)])

    barrier = pltpu.get_barrier_semaphore()

    def greet():
        signal(barrier, sibling)
        if fused:
            signal(barrier, at_x)
            signal(barrier, at_y)

            @pl.when(z < 3)
            def _():
                signal(barrier, at_up)

            @pl.when(z > 0)
            def _():
                signal(barrier, at_down)

    def met():
        peers = 1
        if fused:
            peers = 3 + jnp.where(z < 3, 1, 0) + jnp.where(z > 0, 1, 0)
        pl.semaphore_wait(barrier, peers)


    def remote(kind, c, slot, src, dst, where):
        sem = sem_of(kind, c)
        along = not isinstance(slot, int) or 2 <= slot < 7
        sent = 2 * len(BLOCKS) + kind if along else sem + (len(BLOCKS) if slot == 1 else 0)
        return pltpu.make_async_remote_copy(
            src_ref=src,
            dst_ref=dst,
            send_sem=r.rs_send.at[sent],
            recv_sem=r.rs_recv.at[sem, slot],
            device_id=where,
            device_id_type=MESH,
        )

    def sem_of(kind, c):
        return BLOCKS.index((kind, c))

    def base_of(kind, c):
        return r.base_a.at[c % RING] if kind == ATT else r.base_s

    def before(kind, c):
        return (c - RING) if ATT_SLOTS[0] < ATT_SLOTS[RING] or kind == UP else (c + RING)

    def order_of(kind, c):
        if kind == DOWN:
            return "zx" if c < DOWN_Z else "yxz"
        return "xyz"

    def ordered(kind, c, act):
        if kind != ATT or c < 4:
            act(order_of(kind, c))
            return

        @pl.when(section == 0)
        def _():
            act("xyz")

        @pl.when(section == 1)
        def _():
            act("yxz")

    def first_of(kind, c):
        if kind == SMALL:
            return r.first_s
        return {UP: r.first_u.at[c % RING], DOWN: r.first_d.at[c], ATT: r.first_a.at[c]}[kind]

    def second_of(kind, c):
        if kind == DOWN:
            return r.second_d.at[c - DOWN_Z]
        return r.second_s if kind == SMALL else {UP: r.second_u, ATT: r.second_a}[kind].at[c]

    def z_of(kind, c):
        if kind == DOWN:
            return r.z_d.at[c] if c < DOWN_Z else r.z_d_late.at[c - DOWN_Z]
        return r.z_s if kind == SMALL else {UP: r.z_u, ATT: r.z_a}[kind].at[c]

    def paired(kind, c):
        return kind == UP or (kind == DOWN and c >= DOWN_Z)

    def compute(kind, c):
        both = [c, c + 1]
        if kind in (UP, DOWN):
            if kind == UP:
                part = dot_cols(f_v[...], sl_v[4 * x + c // 2])
                part = part + dot_cols(r.fn_v[...], r.un_v[c // 2])
            else:
                side, q = c // 4, c % 4
                tall = hidden // 32
                at = [
                    (k, slice((2 * i + side) * tall, (2 * i + side + 1) * tall))
                    for k in range(4)
                    for i in range(2)
                ]
                columns = slice(q * LANES, (q + 2) * LANES)
                own = jnp.concatenate([h_v[2 * k + y, :, lanes] for k, lanes in at], axis=1)
                theirs = jnp.concatenate([r.hn_v[k, :, lanes] for k, lanes in at], axis=1)
                part = dot_cols(own, g_v[:, columns]) + dot_cols(theirs, r.gn_v[:, columns])
            for n, k in enumerate(both):
                first = first_of(kind, k)
                block = part[:, n * LANES : (n + 1) * LANES].astype(BF16)
                first[...] = block.reshape(first.shape)
        elif kind == ATT and c == 2:
            part = dot_cols(o_v[...], dz1_v[...]).astype(BF16)
            tall = inner // 16
            for n in range(4):
                base = base_of(kind, c + n // 2)
                block = part[:, n * LANES : (n + 1) * LANES]
                n = n % 2
                base[:, :, :, n * tall : (n + 1) * tall, :] = block.reshape(
                    base.shape[:3] + (tall, LANES)
                )
        elif kind == ATT:
            if c == 0:
                left = j_v[:, pl.ds(patches, latents), :].reshape(rows, width)
                part = dot_cols(left, dq_v[...])
            else:
                keys = images * (patches + latents)
                at = (c - 4) * LANES
                right = kv_v[:, :, at : at + 2 * LANES].reshape(keys, 2 * LANES)
                part = dot_cols(j_v[...].reshape(keys, width), right)
            for n, k in enumerate(both):
                base = base_of(kind, k)
                block = part[:, n * LANES : (n + 1) * LANES].astype(BF16)
                base[...] = block.reshape(base.shape)
        else:
            lines = r.lines[...]
            for j in range(16):
                own = lines[:, j * 64 : (j + 1) * 64]
                value = jnp.concatenate([own[:40], own[40:]], axis=1)
                r.base_s[j // 4, j // 2 % 2, j % 2] = value

    def first_copy(kind, c, order="xyz"):
        base, first = base_of(kind, c), first_of(kind, c)
        if order == "xyz":
            return remote(kind, c, 0, base.at[:, :, 1 - x], first, at_x)
        return remote(kind, c, 0, base.at[:, 1 - y], first, at_y)

    def second_copy(kind, c, order="xyz"):
        first, second = first_of(kind, c), second_of(kind, c)
        if order == "xyz":
            return remote(kind, c, 1, first.at[:, 1 - y], second, at_y)
        return remote(kind, c, 1, first.at[:, 1 - x], second, at_x)

    def end_copy(kind, c):
        if kind == UP:
            return remote(UP, c, 7, r.end_src.at[c], r.end_u.at[c], at_x)
        return remote(DOWN, c, 7, r.z_d.at[c, z, 1 - x], r.end_d.at[c], at_x)

    def begin(kind, c):
        both = [c] if kind == SMALL else [c, c + 1]
        for k in both:
            old = before(kind, k)
            if kind == UP and 0 <= old < CHUNKS:
                second_copy(UP, old).wait_send()
            if kind == ATT and 0 <= old < CHUNKS:
                first_copy(ATT, old).wait_send()
        compute(kind, c)
        for k in both:
            if paired(kind, k):
                second_copy(kind, k, order_of(kind, k)).start()
            elif kind == DOWN:
                z_start(kind, k)
            else:
                ordered(kind, k, lambda order: first_copy(kind, k, order).start())

    def exchange(k, b, src, dst, where):
        return pltpu.make_async_remote_copy(
            src_ref=src,
            dst_ref=dst,
            send_sem=r.pair_send.at[k, b],
            recv_sem=r.pair_recv.at[k, b],
            device_id=where,
            device_id_type=MESH,
        )

    def span_of(b):
        return pl.ds(pl.multiple_of(b * per, per), per)

    def exchange_f(b):
        return exchange(0, b, f_v.at[span_of(b)], r.fn_v.at[span_of(b)], at_x)

    def exchange_u(b):
        src = sl_v.at[pl.ds(4 * (1 - x), 4), span_of(b)]
        return exchange(1, b, src, r.un_v.at[:, span_of(b)], at_x)

    def exchange_g(b):
        return exchange(2, b, g_v.at[span_of(b)], r.gn_v.at[span_of(b)], at_y)

    def exchange_h(b):
        src = h_v.reshape(4, 2, rows, STEP).at[:, 1 - y, span_of(b)]
        return exchange(3, b, src, r.hn_v.at[:, span_of(b)], at_y)


    def phase_one(wq_v, wo_v, wu_v, wd_v, z_v, q_v, p_v, z1_v, y_v, acc, do_v, mask_v):
        greet()
        loads = [
            load(0, r.wkv, wkv_v),
            load(1, r.wq, wq_v),
            load(2, r.wo, wo_v),
            load(3, r.wu, wu_v),
            load(4, r.wd, wd_v),
        ]
        media_load(0).start()
        loads[0].start()
        for i in range(1, images):
            media_load(i).start()
        for copy in loads[1:]:
            copy.start()
        g_load = load(5, r.cotangent, g_v)

        def start_load(i):
            return load(6 + images, r.start, z_v.at[pl.ds(i * latents, latents)])

        @pl.when(section == 0)
        def _():
            for i in range(images):
                start_load(i).start()

        @pl.when(section == 1)
        def _():
            g_load.start()

        row_head = lax.broadcasted_iota(jnp.int32, (heads * latents, LANES), 0) // latents
        lane_head = lax.broadcasted_iota(jnp.int32, (heads * latents, LANES), 1) // HEAD_DIM
        mask_v[...] = jnp.where(row_head == lane_head, 1.0, 0.0).astype(BF16)
        r.lines[...] = jnp.zeros_like(r.lines)

        loads[0].wait()

        pieces = 4
        tall = patches // pieces
        wide = 2 * inner // pieces

        def media_piece(i, n):
            span = slice(n * tall, (n + 1) * tall)
            hat, _ = normed(j_v[i, span, :].astype(F32))
            low = (hat * r.media_gain[...] + r.media_bias[...]).astype(BF16)
            j_v[i, span, :] = low
            return low

        def media_all():
            media_load(0).wait()
            low = jnp.concatenate([media_piece(0, n) for n in range(pieces)], axis=0)
            for i in range(images):
                later = []
                if i + 1 < images:
                    media_load(i + 1).wait()
                for n in range(pieces):
                    lanes = slice(n * wide, (n + 1) * wide)
                    kv_v[i, :patches, lanes] = dot(low, wkv_v[:, lanes]).astype(BF16)
                    if i + 1 < images:
                        later.append(media_piece(i + 1, n))
                if later:
                    low = jnp.concatenate(later, axis=0)

        media_all()
        for copy in loads[1:]:
            copy.wait()

        @pl.when(section == 0)
        def _():
            load(6 + images, z_v, z_v).wait()

        @pl.when(section == 1)
        def _():
            g_load.wait()
            for i in range(images):
                span = slice(i * latents, (i + 1) * latents)
                live = r.live[i].astype(F32)
                g_v[span, :] = (g_v[span, :].astype(F32) * live).astype(BF16)

        met()
        if fused:

            @pl.when(section == 1)
            def _():
                for b in range(batches):
                    exchange_g(b).start()


        def relay_latents(b):
            span = pl.ds(b * per, per)
            return pltpu.make_async_remote_copy(
                src_ref=y_v.at[span],
                dst_ref=z_v.at[span],
                send_sem=r.send_sem.at[b],
                recv_sem=r.recv_sem.at[b],
                device_id=sibling,
                device_id_type=MESH,
            )

        def relay_grad(b):
            span = pl.ds(b * per, per)
            return pltpu.make_async_remote_copy(
                src_ref=y_v.at[span],
                dst_ref=g_v.at[span],
                send_sem=r.send_sem.at[batches + b],
                recv_sem=r.recv_sem.at[batches + b],
                device_id=sibling,
                device_id_type=MESH,
            )

        def spread(block):
            return jnp.concatenate([block] * heads, axis=0) * mask_v[...]

        def gathered(block):
            lane = lax.broadcasted_iota(jnp.int32, (latents, LANES), 1) // HEAD_DIM
            total = block[0:latents]
            for k in range(1, heads):
                total = jnp.where(lane == k, block[k * latents : (k + 1) * latents], total)
            return total

        def chains(i, local):
            for k in range(TOGETHER):
                at = pl.ds(pl.multiple_of((i + k) * latents, latents), latents)
                here = slice((local + k) * latents, (local + k + 1) * latents)
                for n in range(groups):
                    lanes = slice(n * LANES, (n + 1) * LANES)
                    values = slice(inner + n * LANES, inner + (n + 1) * LANES)
                    yield i + k, (i + k) * groups + n, at, here, lanes, values

        def attend(i):
            todo = list(chains(i, 0))
            scores = [
                dot_rows(kv_v[img, :, lanes], spread(q_v[at, lanes]))
                for img, _, at, _, lanes, _ in todo
            ]
            e = [jnp.exp(s - jnp.max(s, axis=0, keepdims=True)) for s in scores]
            prob = [(v * (1.0 / jnp.sum(v, axis=0, keepdims=True))).astype(BF16) for v in e]
            for (_, slot, *_), p in zip(todo, prob):
                p_v[slot] = p
            mixed = [dot_cols(p, kv_v[img, :, values]) for (img, *_, values), p in zip(todo, prob)]
            for (_, _, at, _, lanes, _), o in zip(todo, mixed):
                o_v[at, lanes] = gathered(o).astype(BF16)

        def attend_back(i, local):
            todo = list(chains(i, local))
            wide = [spread(do_v[here, lanes]) for _, _, _, here, lanes, _ in todo]
            dprob = [dot_rows(kv_v[c[0], :, c[5]], w) for c, w in zip(todo, wide)]
            dv = [dot(p_v[c[1]], w) for c, w in zip(todo, wide)]
            ds = []
            for c, d in zip(todo, dprob):
                p = p_v[c[1]].astype(F32)
                t = p * d
                ds.append((t - p * jnp.sum(t, axis=0, keepdims=True)).astype(BF16))
            query = [spread(q_v[at, lanes]) for _, _, at, _, lanes, _ in todo]
            dq = [dot_cols(d, kv_v[c[0], :, c[4]]) for c, d in zip(todo, ds)]
            dk = [dot(d, q) for d, q in zip(ds, query)]
            for (img, _, at, _, lanes, values), dq_, dk_, dv_ in zip(todo, dq, dk, dv):
                dq_v[at, lanes] = gathered(dq_).astype(BF16) * BF16(HEAD_DIM**-0.5)
                kv_v[img, :, lanes] = dk_.astype(BF16)
                kv_v[img, :, values] = dv_.astype(BF16)

        def forward(b, carry):
            span = pl.ds(pl.multiple_of(b * per, per), per)

            @pl.when(section == 1)
            def _():
                relay_latents(b).wait_recv()

            zed = z_v[span, :].astype(F32)
            hat, _ = normed(zed)
            low = (hat * r.latent_gain[...] + r.latent_bias[...]).astype(BF16)
            j_v[pl.ds(b * GROUP, GROUP), pl.ds(patches, latents), :] = low.reshape(
                GROUP, latents, width
            )
            q_v[span, :] = (dot(low, wq_v[...]) * HEAD_DIM**-0.5).astype(BF16)
            kv_v[pl.ds(b * GROUP, GROUP), pl.ds(patches, latents), :] = (
                dot(low, wkv_v[...]).astype(BF16).reshape(GROUP, latents, 2 * inner)
            )

            for k in range(0, GROUP, TOGETHER):
                attend(b * GROUP + k)
            mixed = zed + dot(o_v[span, :], wo_v[...])
            z1_v[span, :] = mixed
            hat, _ = normed(mixed)
            low = (hat * r.ff_gain[...] + r.ff_bias[...]).astype(BF16)
            f_v[span, :] = low
            if fused:
                exchange_f(b).start()
            u = dot(low, wu_v[:, 0:STEP])
            for c in range(chunks):
                lanes = slice(c * STEP, (c + 1) * STEP)
                later = None
                if c + 1 < chunks:
                    later = dot(low, wu_v[:, (c + 1) * STEP : (c + 2) * STEP])
                h, slope = gelu_and_slope(u)
                h = h.astype(BF16)
                h_v[c, span, :] = h
                sl_v[c, span, :] = slope.astype(BF16)
                part = dot(h, wd_v[lanes, :])
                acc[...] = part + (mixed if c == 0 else acc[...])
                u = later
            y_v[span, :] = acc[...].astype(BF16)

            @pl.when(section == 0)
            def _():
                relay_latents(b).start()

            if fused:
                @pl.when((section == 1) | (b + 1 < batches))
                def _():
                    exchange_h(b).start()

            return carry

        lax.fori_loop(0, batches, forward, 0)
        y_store = store(0, y_v, r.y_out)
        y_store.start()

        def backward_ff(b, carry):
            span = pl.ds(pl.multiple_of(b * per, per), per)

            @pl.when(section == 0)
            def _():
                if fused:

                    @pl.when(b == 0)
                    def _():
                        pl.semaphore_wait(r.go, 1)
                        exchange_h(batches - 1).start()

                relay_grad(b).wait_recv()
                if fused:
                    exchange_g(b).start()

            g = g_v[span, :]

            def chunk(n):
                return lax.rem(n + chunks // 2 * (1 - x), chunks)

            def part_of(n):
                return pl.ds(pl.multiple_of(chunk(n) * STEP, STEP), STEP)

            dh = dot_rows(g, wd_v[part_of(0), :])
            for n in range(chunks):
                later = None
                if n + 1 < chunks:
                    later = dot_rows(g, wd_v[part_of(n + 1), :])
                du = (dh * sl_v[chunk(n), span, :].astype(F32)).astype(BF16)
                sl_v[chunk(n), span, :] = du
                part = dot_rows(du, wu_v[:, part_of(n)])
                acc[...] = part if n == 0 else acc[...] + part
                dh = later
                if fused and n + 1 == chunks // 2:
                    exchange_u(b).start()
            if fused:
                @pl.when((section == 1) & (b == 0))
                def _():
                    signal(r.go, sibling)

            df = acc[...]
            hat, factor = normed(z1_v[span, :])
            r.lines[4:5, :] += jnp.sum(df * hat, axis=0, keepdims=True)
            r.lines[5:6, :] += jnp.sum(df, axis=0, keepdims=True)
            dz1 = g.astype(F32) + norm_back(df, hat, factor, r.ff_gain[...])
            z1_v[span, :] = dz1
            dz1_v[span, :] = dz1.astype(BF16)
            return carry

        def backward_attention(b, carry):
            span = pl.ds(pl.multiple_of(b * per, per), per)
            do_v[...] = dot_rows(dz1_v[span, :], wo_v[...]).astype(BF16)

            for k in range(0, GROUP, TOGETHER):
                attend_back(b * GROUP + k, k)
            tail = kv_v[pl.ds(b * GROUP, GROUP), pl.ds(patches, latents), :].reshape(per, 2 * inner)
            dn = dot_rows(dq_v[span, :], wq_v[...]) + dot_rows(tail, wkv_v[...])
            hat, factor = normed(z_v[span, :].astype(F32))
            r.lines[2:3, :] += jnp.sum(dn * hat, axis=0, keepdims=True)
            r.lines[3:4, :] += jnp.sum(dn, axis=0, keepdims=True)
            dz = z1_v[span, :] + norm_back(dn, hat, factor, r.latent_gain[...])
            y_v[span, :] = dz.astype(BF16)

            @pl.when(section == 1)
            def _():
                relay_grad(b).start()

            @pl.when(section == 0)
            def _():
                total = dz[0:latents]
                for k in range(1, GROUP):
                    total = total + dz[k * latents : (k + 1) * latents]
                r.lines[8 : 8 + latents, :] += total

            return carry

        y_store.wait()

        @pl.when(section == 0)
        def _():
            for b in range(batches):
                relay_latents(b).wait_send()

        def backward(b, carry):
            return backward_attention(b, backward_ff(b, carry))

        lax.fori_loop(0, batches, backward, 0)

        @pl.when(section == 1)
        def _():
            for b in range(batches):
                relay_grad(b).wait_send()

    pl.run_scoped(
        phase_one,
        pltpu.VMEM(r.wq.shape, BF16),
        pltpu.VMEM(r.wo.shape, BF16),
        pltpu.VMEM(r.wu.shape, BF16),
        pltpu.VMEM(r.wd.shape, BF16),
        pltpu.VMEM((rows, width), BF16),
        pltpu.VMEM((rows, inner), BF16),
        pltpu.VMEM((images * groups, patches + latents, heads * latents), BF16),
        pltpu.VMEM((rows, width), F32),
        pltpu.VMEM((rows, width), BF16),
        pltpu.VMEM((per, width), F32),
        pltpu.VMEM((per, inner), BF16),
        pltpu.VMEM((heads * latents, LANES), BF16),
    )

    if not fused:
        copies = [
            store(k + 1, src, dst)
            for k, (src, dst) in enumerate(
                [
                    (j_v, r.j_out),
                    (kv_v, r.kv_out),
                    (o_v, r.o_out),
                    (f_v, r.f_out),
                    (h_v, r.h_out),
                    (sl_v, r.du_out),
                    (dz1_v, r.dz1_out),
                    (dq_v, r.dq_out),
                    (g_v, r.g_out),
                ]
            )
        ]
        for copy in copies:
            copy.start()
        for copy in copies:
            copy.wait()
        r.lines_out[...] = r.lines[...]
        return


    def z_base(kind, c):
        return first_of(kind, c) if order_of(kind, c) == "zx" else second_of(kind, c)

    def up_copy(kind, c, d, src):
        return remote(kind, c, 2 + d, src, z_of(kind, c).at[d], at_up)

    def down_copy(kind, c, d, src, last):
        place = 4 if last else d
        return remote(kind, c, 2 + place, src, z_of(kind, c).at[place], at_down)

    def add_into(dst, src):
        lead = dst.shape[:-2]
        if not lead:
            dst[...] = halves(dst[...], src[...])
            return
        total = 1
        for size in lead:
            total *= size

        def step(k, carry):
            at = []
            for size in reversed(lead):
                at.append(lax.rem(k, size))
                k = k // size
            at = tuple(reversed(at))
            dst[at] = halves(dst[at], src[at])
            return carry

        lax.fori_loop(0, total, step, 0)

    def send_own(kind, c, d, up):
        src = z_base(kind, c).at[d]
        if up:
            up_copy(kind, c, d, src).start()
        else:
            down_copy(kind, c, d, src, d == 2).start()

    def pass_on(kind, c, d, up, last=False):
        zb = z_of(kind, c)
        up_copy(kind, c, d, zb.at[d]).wait_recv()
        add_into(zb.at[d], z_base(kind, c).at[d])
        if up:
            up_copy(kind, c, d, zb.at[d]).start()
        else:
            down_copy(kind, c, d, zb.at[d], last).start()

    def z_start(kind, c):
        zb = z_of(kind, c)

        @pl.when(z == 0)
        def _():
            zb[0] = jnp.zeros(zb.shape[1:], zb.dtype)
            send_own(kind, c, 3, True)

        @pl.when(z == 3)
        def _():
            zb[4] = jnp.zeros(zb.shape[1:], zb.dtype)
            send_own(kind, c, 0, False)

    def z_near(kind, c):
        @pl.when(z == 0)
        def _():
            send_own(kind, c, 2, True)

        @pl.when(z == 1)
        def _():
            pass_on(kind, c, 3, True)

        @pl.when(z == 2)
        def _():
            pass_on(kind, c, 0, False)

        @pl.when(z == 3)
        def _():
            send_own(kind, c, 1, False)

    def z_far(kind, c):
        @pl.when(z == 0)
        def _():
            send_own(kind, c, 1, True)

        @pl.when(z == 1)
        def _():
            pass_on(kind, c, 0, False, True)
            pass_on(kind, c, 2, True)

        @pl.when(z == 2)
        def _():
            pass_on(kind, c, 3, True)
            pass_on(kind, c, 1, False, True)

        @pl.when(z == 3)
        def _():
            send_own(kind, c, 2, False)

    def z_arrive(kind, c):
        zb = z_of(kind, c)

        @pl.when(z > 0)
        def _():
            remote(kind, c, 2 + z, zb.at[z], zb.at[z], at_up).wait_recv()

        @pl.when(z < 3)
        def _():
            remote(kind, c, 6, zb.at[4], zb.at[4], at_down).wait_recv()

    def finish(kind, c, total):
        def put(k, rows_at, lanes_at, value):
            held, out = results()[k]
            held[rows_at, lanes_at] = value
            out_copy(held.at[rows_at, lanes_at], out.at[rows_at, lanes_at], k).start()

        tall = total.shape[0]
        if kind == DOWN:
            rows_at, lanes_at = down_at(c)
            put(1, rows_at, lanes_at, total)
        elif kind == ATT and c < 2:
            put(2, slice(0, tall), slice(c * LANES, (c + 1) * LANES), total)
        elif kind == ATT and c < 4:
            tall = tall // 2
            for n in range(2):
                at = ((c - 2) * 2 + n) * LANES
                value = total[n * tall : (n + 1) * tall]
                put(3, slice(0, tall), slice(at, at + LANES), value)
        elif kind == ATT:
            at = (c - 4) * LANES
            put(4, slice(0, tall), slice(at, at + LANES), total)
        else:
            r.small_out[...] = total

            @pl.when(section == 0)
            def _():
                relay_start().start()
                own_start().start()

    def relay_start():
        last = 2 * batches + images
        return pltpu.make_async_remote_copy(
            src_ref=r.small_out,
            dst_ref=r.start_out,
            send_sem=r.send_sem.at[last],
            recv_sem=r.recv_sem.at[last],
            device_id=sibling,
            device_id_type=MESH,
        )

    def own_start():
        return store(9, r.small_out, r.start_out)

    def results():
        return (
            (r.up_out, r.up_out),
            (r.down_v, r.down_out),
            (r.query_v, r.query_out),
            (r.out_v, r.out_out),
            (r.keyval_v, r.keyval_out),
        )

    def out_copy(src, dst, k):
        return pltpu.make_async_copy(src, dst, r.out_sem.at[k])

    def down_at(c):
        tall = hidden // 32
        return slice(c // 4 * tall, (c // 4 + 1) * tall), slice(c % 4 * LANES, (c % 4 + 1) * LANES)

    def put_up(c, n, half, total):
        held = r.up_v.at[n, :, pl.ds(c * LANES, LANES)]
        held[...] = total
        at = pl.multiple_of(half * (hidden // 2) + c * LANES, LANES)
        out_copy(held, r.up_out.at[:, pl.ds(at, LANES)], 0).start()

    def advance(kind, c, step):
        zb = z_of(kind, c)
        if kind == DOWN and c < DOWN_Z:
            base = first_of(kind, c)
            if step == 1:
                z_near(kind, c)
            elif step == 2:
                z_far(kind, c)
            elif step == 3:
                z_arrive(kind, c)
                total = base[z, 1 - x].astype(F32) + zb[z, 1 - x].astype(F32)
                zb[z, 1 - x] = (total + zb[4, 1 - x].astype(F32)).astype(BF16)
                end_copy(kind, c).start()
                total = base[z, x].astype(F32) + zb[z, x].astype(F32)
                r.down_v[down_at(c)] = total + zb[4, x].astype(F32)
            elif step == 4:
                end_copy(kind, c).wait_recv()
                finish(kind, c, r.down_v[down_at(c)] + r.end_d[c].astype(F32))
            return
        first, second = first_of(kind, c), second_of(kind, c)

        def add_first(order):
            base = base_of(kind, c)
            add_into(first, base.at[:, :, x] if order == "xyz" else base.at[:, y])
            second_copy(kind, c, order).start()

        def add_second(order):
            add_into(second, first.at[:, y] if order == "xyz" else first.at[:, x])

        if step == 1:
            first_copy(kind, c).wait_recv()
            ordered(kind, c, add_first)
        elif step == 2:
            second_copy(kind, c).wait_recv()
            ordered(kind, c, add_second)
            z_start(kind, c)
        elif step == 3:
            z_near(kind, c)
        elif step == 4:
            z_far(kind, c)
        elif step == 5 and kind == UP:
            z_arrive(kind, c)
            total = second[z, 1 - x].astype(F32) + zb[z, 1 - x].astype(F32)
            r.end_src[c] = (total + zb[4, 1 - x].astype(F32)).astype(BF16)
            end_copy(kind, c).start()
            total = second[z, x].astype(F32) + zb[z, x].astype(F32)
            put_up(c, 0, x, total + zb[4, x].astype(F32))
        elif step == 5:
            z_arrive(kind, c)
            total = second[z].astype(F32) + zb[z].astype(F32)
            finish(kind, c, total + zb[4].astype(F32))
        elif step == 6 and kind == UP:
            end_copy(kind, c).wait_recv()
            put_up(c, 1, 1 - x, r.end_u[c].astype(F32))

    def sends_done():
        for kind, c in BLOCKS:
            taken = 0 <= 2 * c - before(kind, c) < CHUNKS
            if kind == SMALL or (kind == ATT and not taken):
                first_copy(kind, c).wait_send()
            if not (kind == DOWN and c < DOWN_Z) and not (kind == UP and taken):
                second_copy(kind, c).wait_send()
            if kind == UP or (kind == DOWN and c < DOWN_Z):
                end_copy(kind, c).wait_send()
        for kind, along in (
            (UP, r.z_u),
            (DOWN, r.z_d),
            (DOWN, r.z_d_late),
            (ATT, r.z_a),
            (SMALL, r.z_s),
        ):
            along = along.at[0:3] if kind == SMALL else along.at[:, 0:3]
            remote(kind, 0, 2, along, along, at_x).wait_send()
        for b in range(batches):
            for copy in (exchange_f(b), exchange_u(b), exchange_g(b), exchange_h(b)):
                copy.wait_send()

    def phase_two(*buffers):
        names_two = ["first_u", "second_u", "z_u", "end_src", "end_u", "first_d"]
        names_two += ["second_d", "z_d", "z_d_late", "end_d"]
        names_two += ["base_a", "first_a", "second_a", "z_a"]
        names_two += ["base_s", "first_s", "second_s", "z_s", "media_v", "mine_v", "other_v"]
        names_two += ["up_v", "down_v", "keyval_v", "query_v", "out_v"]
        r.__dict__.update(zip(names_two, buffers, strict=True))
        media_v, mine_v, other_v = r.media_v, r.mine_v, r.other_v

        signal(r.ready.at[0], at_x)
        signal(r.ready.at[1], at_y)

        @pl.when(z < 3)
        def _():
            signal(r.ready.at[2], at_up)

        @pl.when(z > 0)
        def _():
            signal(r.ready.at[3], at_down)

        def urgency(entry):
            step, kind, c = entry
            return step == final(kind, c), final(kind, c) - step, kind, c

        def image_load(i):
            return load(6 + i, r.media.at[i], media_v.at[i % 2])

        def mine_store(i):
            return store(1 + i, mine_v, r.mine_out.at[i])

        def relay_media(i):
            return pltpu.make_async_remote_copy(
                src_ref=other_v.at[i % 2],
                dst_ref=r.theirs_out.at[i],
                send_sem=r.send_sem.at[2 * batches + i],
                recv_sem=r.recv_sem.at[2 * batches + i],
                device_id=sibling,
                device_id_type=MESH,
            )

        def media_grad(i):
            half = width // 2
            image_load(i).wait()
            dj = dot_rows(kv_v[i, pl.ds(0, patches), :], wkv_v[...])
            hat, factor = normed(media_v[i % 2].astype(F32))
            r.lines[0:1, :] += jnp.sum(dj * hat, axis=0, keepdims=True)
            r.lines[1:2, :] += jnp.sum(dj, axis=0, keepdims=True)
            grad = norm_back(dj, hat, factor, r.media_gain[...])
            if i >= 1:
                mine_store(i - 1).wait()
            if i >= 2:
                relay_media(i - 2).wait_send()

            @pl.when(section == 0)
            def _():
                mine_v[...] = grad[:, :half]
                other_v[i % 2] = grad[:, half:].astype(BF16)

            @pl.when(section == 1)
            def _():
                mine_v[...] = grad[:, half:]
                other_v[i % 2] = grad[:, :half].astype(BF16)

            mine_store(i).start()
            relay_media(i).start()
            if i + 2 < images:
                image_load(i + 2).start()

        image_load(0).start()
        image_load(1).start()
        pl.semaphore_wait(r.ready.at[0], 1)
        pl.semaphore_wait(r.ready.at[1], 1)

        @pl.when(z > 0)
        def _():
            pl.semaphore_wait(r.ready.at[2], 1)

        @pl.when(z < 3)
        def _():
            pl.semaphore_wait(r.ready.at[3], 1)

        slots = {(SMALL, 0): SMALL_SLOT}
        for kind, at in ((DOWN, DOWN_SLOTS), (ATT, ATT_SLOTS), (UP, UP_SLOTS)):
            slots.update({(kind, c): slot for c, slot in enumerate(at)})
        last = max(slots.values()) + 7
        for b in range(batches):
            exchange_g(b).wait_recv()
            exchange_h(b).wait_recv()

        def final(kind, c):
            return 6 if kind == UP else 4 if kind == DOWN and c < DOWN_Z else 5

        def slot_of(kind, c, step):
            return slots[kind, c] + step - paired(kind, c)

        for slot in range(last):
            for (kind, c), at in slots.items():
                if at == slot and c % 2 == 0:
                    if kind == UP and c == 0:
                        for b in range(batches):
                            exchange_f(b).wait_recv()
                            exchange_u(b).wait_recv()
                    begin(kind, c)
            live = []
            for kind, c in slots:
                steps = range(1 + paired(kind, c), final(kind, c) + 1)
                live += [(n, kind, c) for n in steps if slot_of(kind, c, n) == slot]
            for step, kind, c in sorted(live, key=urgency):
                advance(kind, c, step)
            for i in range(images):
                if MEDIA_SLOTS[i] == slot:
                    media_grad(i)

        sends_done()
        mine_store(images - 1).wait()
        for i in range(images - 2, images):
            relay_media(i).wait_send()
        for i in range(images):
            relay_media(i).wait_recv()
        for k, (held, out) in enumerate(results()):
            out_copy(held, out, k).wait()

        @pl.when(section == 0)
        def _():
            relay_start().wait_send()
            own_start().wait()

        @pl.when(section == 1)
        def _():
            relay_start().wait_recv()

    tile_u, tile_d = (width // 16, LANES), (hidden // 32, LANES)
    tile_a, tile_s = (width // 16, LANES), (40, 128)
    pl.run_scoped(
        phase_two,
        pltpu.VMEM((RING, 4, 2, 2) + tile_u, BF16),
        pltpu.VMEM((CHUNKS, 4, 2) + tile_u, BF16),
        pltpu.VMEM((CHUNKS, 5, 2) + tile_u, BF16),
        pltpu.VMEM((CHUNKS,) + tile_u, BF16),
        pltpu.VMEM((CHUNKS,) + tile_u, BF16),
        pltpu.VMEM((CHUNKS, 4, 2) + tile_d, BF16),
        pltpu.VMEM((CHUNKS - DOWN_Z, 4) + tile_d, BF16),
        pltpu.VMEM((DOWN_Z, 5, 2) + tile_d, BF16),
        pltpu.VMEM((CHUNKS - DOWN_Z, 5) + tile_d, BF16),
        pltpu.VMEM((DOWN_Z,) + tile_d, BF16),
        pltpu.VMEM((RING, 4, 2, 2) + tile_a, BF16),
        pltpu.VMEM((CHUNKS, 4, 2) + tile_a, BF16),
        pltpu.VMEM((CHUNKS, 4) + tile_a, BF16),
        pltpu.VMEM((CHUNKS, 5) + tile_a, BF16),
        pltpu.VMEM((4, 2, 2) + tile_s, F32),
        pltpu.VMEM((4, 2) + tile_s, F32),
        pltpu.VMEM((4,) + tile_s, F32),
        pltpu.VMEM((5,) + tile_s, F32),
        pltpu.VMEM((2, patches, width), BF16),
        pltpu.VMEM((patches, width // 2), F32),
        pltpu.VMEM((2, patches, width // 2), BF16),
        pltpu.VMEM((2, width // 16, hidden // 2), F32),
        pltpu.VMEM((hidden // 16, width), F32),
        pltpu.VMEM((width // 16, 2 * inner), F32),
        pltpu.VMEM((width // 16, inner), F32),
        pltpu.VMEM((inner // 16, width), F32),
    )


def layers(fused, start, media, cotangent, live, lines, wq, wkv, wo, wu, wd):
    images, patches, width = media.shape
    latents = start.shape[0]
    inner = wq.shape[1]
    hidden = wu.shape[1]
    rows = images * latents
    batches = images // GROUP
    dims = (images, latents, patches, inner, hidden, width)
    keys = patches + latents
    any_spec = pl.BlockSpec(memory_space=pl.ANY)
    vmem_spec = pl.BlockSpec(memory_space=pltpu.VMEM)
    smem_spec = pl.BlockSpec(memory_space=pltpu.SMEM)

    def low(*shape):
        return jax.ShapeDtypeStruct(shape, BF16)

    def full(*shape):
        return jax.ShapeDtypeStruct(shape, F32)

    ins = [
        ("start", start, any_spec),
        ("media", media, any_spec),
        ("cotangent", cotangent, any_spec),
        ("live", live, smem_spec),
    ]
    line_names = ["media_gain", "media_bias", "latent_gain", "latent_bias", "ff_gain", "ff_bias"]
    ins += [(n, a, vmem_spec) for n, a in zip(line_names, lines, strict=True)]
    ins += [(n, a, any_spec) for n, a in zip(("wq", "wkv", "wo", "wu", "wd"), (wq, wkv, wo, wu, wd))]
    outs = [("y_out", low(rows, width), any_spec)]
    if fused:
        outs += [
            ("mine_out", full(images, patches, width // 2), any_spec),
            ("theirs_out", low(images, patches, width // 2), any_spec),
            ("up_out", full(width // 16, hidden), any_spec),
            ("down_out", full(hidden // 16, width), any_spec),
            ("keyval_out", full(width // 16, 2 * inner), any_spec),
            ("query_out", full(width // 16, inner), any_spec),
            ("out_out", full(inner // 16, width), any_spec),
            ("start_out", full(40, 128), any_spec),
            ("small_out", full(40, 128), vmem_spec),
        ]
    else:
        outs += [
            ("j_out", low(images, keys, width), any_spec),
            ("kv_out", low(images, keys, 2 * inner), any_spec),
            ("o_out", low(rows, inner), any_spec),
            ("f_out", low(rows, width), any_spec),
            ("h_out", low(hidden // STEP, rows, STEP), any_spec),
            ("du_out", low(hidden // STEP, rows, STEP), any_spec),
            ("dz1_out", low(rows, width), any_spec),
            ("dq_out", low(rows, inner), any_spec),
            ("g_out", low(rows, width), any_spec),
            ("lines_out", full(80, width), vmem_spec),
        ]
    scratch = [
        ("wkv_v", pltpu.VMEM(wkv.shape, BF16)),
        ("j_v", pltpu.VMEM((images, keys, width), BF16)),
        ("kv_v", pltpu.VMEM((images, keys, 2 * inner), BF16)),
        ("o_v", pltpu.VMEM((rows, inner), BF16)),
        ("f_v", pltpu.VMEM((rows, width), BF16)),
        ("h_v", pltpu.VMEM((hidden // STEP, rows, STEP), BF16)),
        ("sl_v", pltpu.VMEM((hidden // STEP, rows, STEP), BF16)),
        ("g_v", pltpu.VMEM((rows, width), BF16)),
        ("dz1_v", pltpu.VMEM((rows, width), BF16)),
        ("dq_v", pltpu.VMEM((rows, inner), BF16)),
        ("lines", pltpu.VMEM((80, width), F32)),
        ("load_sem", pltpu.SemaphoreType.DMA((7 + images,))),
        ("store_sem", pltpu.SemaphoreType.DMA((10,))),
        ("send_sem", pltpu.SemaphoreType.DMA((2 * batches + images + 1,))),
        ("recv_sem", pltpu.SemaphoreType.DMA((2 * batches + images + 1,))),
    ]
    if fused:
        scratch += [
            ("hn_v", pltpu.VMEM((4, rows, STEP), BF16)),
            ("gn_v", pltpu.VMEM((rows, width), BF16)),
            ("fn_v", pltpu.VMEM((rows, width), BF16)),
            ("un_v", pltpu.VMEM((4, rows, STEP), BF16)),
            ("pair_send", pltpu.SemaphoreType.DMA((4, batches))),
            ("pair_recv", pltpu.SemaphoreType.DMA((4, batches))),
            ("rs_send", pltpu.SemaphoreType.DMA((2 * len(BLOCKS) + 5,))),
            ("rs_recv", pltpu.SemaphoreType.DMA((len(BLOCKS), 8))),
            ("out_sem", pltpu.SemaphoreType.DMA((5,))),
            ("go", pltpu.SemaphoreType.REGULAR),
            ("ready", pltpu.SemaphoreType.REGULAR((4,))),
        ]
    names = [n for n, *_ in ins] + [n for n, *_ in outs] + [n for n, _ in scratch]
    results = pl.pallas_call(
        functools.partial(layer_kernel, dims, fused, names),
        out_shape=[s for _, s, _ in outs],
        in_specs=[s for _, _, s in ins],
        out_specs=[s for _, _, s in outs],
        scratch_shapes=[s for _, s in scratch],
        compiler_params=pltpu.CompilerParams(
            collective_id=1, has_side_effects=True, vmem_limit_bytes=VMEM_LIMIT
        ),
        name="layers",
    )(*[a for _, a, _ in ins])
    return Refs([n for n, *_ in outs], results)


def media_kernel(dims, dkv, media, wkv, gain, mine, other, sums):
    patches, half = dims
    section = lax.axis_index("section")

    @pl.when(pl.program_id(0) == 0)
    def _():
        sums[...] = jnp.zeros_like(sums)

    dj = dot_rows(dkv[0], wkv[...])
    hat, factor = normed(media[0].astype(F32))
    sums[0:1, :] += jnp.sum(dj * hat, axis=0, keepdims=True)
    sums[1:2, :] += jnp.sum(dj, axis=0, keepdims=True)
    grad = norm_back(dj, hat, factor, gain[...])

    @pl.when(section == 0)
    def _():
        mine[0] = grad[:, :half]
        other[0] = grad[:, half:].astype(BF16)

    @pl.when(section == 1)
    def _():
        mine[0] = grad[:, half:]
        other[0] = grad[:, :half].astype(BF16)


def media_grads(dkv, media, wkv, gain):
    images, patches, width = media.shape
    half = width // 2
    return pl.pallas_call(
        functools.partial(media_kernel, (patches, half)),
        grid=(images,),
        out_shape=[
            jax.ShapeDtypeStruct((images, patches, half), F32),
            jax.ShapeDtypeStruct((images, patches, half), BF16),
            jax.ShapeDtypeStruct((8, width), F32),
        ],
        in_specs=[
            pl.BlockSpec((1, patches, dkv.shape[2]), lambda i: (i, 0, 0)),
            pl.BlockSpec((1, patches, width), lambda i: (i, 0, 0)),
            pl.BlockSpec(wkv.shape, lambda i: (0, 0)),
            pl.BlockSpec((1, width), lambda i: (0, 0)),
        ],
        out_specs=[
            pl.BlockSpec((1, patches, half), lambda i: (i, 0, 0)),
            pl.BlockSpec((1, patches, half), lambda i: (i, 0, 0)),
            pl.BlockSpec((8, width), lambda i: (0, 0)),
        ],
        compiler_params=pltpu.CompilerParams(vmem_limit_bytes=48 * 1024 * 1024),
        name="media_grads",
    )(dkv, media, wkv, gain)


def hand_over_kernel(latents, mine, theirs, small, start, *refs):
    count = (len(refs) - 8) // 2
    sources, media_out, start_out = refs[:count], refs[count], refs[count + 1]
    lines, targets = refs[count + 2 : count + 8], refs[count + 8 :]
    section = lax.axis_index("section")

    @pl.when(pl.program_id(0) == 0)
    def _():
        for k, line in enumerate(lines):
            line[...] = small[k : k + 1, :64]

        @pl.when(section == 0)
        def _():
            start_out[...] = start[8 : 8 + latents // 2, :64]

        @pl.when(section == 1)
        def _():
            start_out[...] = start[: latents // 2, 64:]

    media_out[...] = mine[...] + theirs[...].astype(F32)
    for source, target in zip(sources, targets):
        target[...] = source[...]


def hand_over(latents, mine, theirs, small, start, arrays):
    images, patches, half = mine.shape
    steps = 4
    media_spec = pl.BlockSpec((images // steps, patches, half), lambda i: (i, 0, 0))

    def whole(shape):
        return pl.BlockSpec(shape, lambda i: (0, 0))

    line, start_shape = (1, 64), (latents // 2, 64)
    parts = [
        pl.BlockSpec((a.shape[0] // steps, a.shape[1]), lambda i: (i, 0))
        if a.shape[0] % (8 * steps) == 0
        else whole(a.shape)
        for a in arrays
    ]
    return pl.pallas_call(
        functools.partial(hand_over_kernel, latents),
        grid=(steps,),
        out_shape=[jax.ShapeDtypeStruct(mine.shape, F32), jax.ShapeDtypeStruct(start_shape, F32)]
        + [jax.ShapeDtypeStruct(line, F32)] * 6
        + [jax.ShapeDtypeStruct(a.shape, a.dtype) for a in arrays],
        in_specs=[media_spec, media_spec, whole(small.shape), whole(start.shape)] + parts,
        out_specs=[media_spec, whole(start_shape)] + [whole(line)] * 6 + parts,
        compiler_params=pltpu.CompilerParams(vmem_limit_bytes=VMEM_LIMIT),
        name="hand_over",
    )(mine, theirs, small, start, *arrays)


def weight_grad(left, right):
    left = left.reshape(-1, left.shape[-1])
    right = right.reshape(-1, right.shape[-1])
    return dot_cols(left, right).astype(BF16)


def swap_sections(value):
    return lax.ppermute(value, "section", [(0, 1), (1, 0)])


def shards(
    media,
    image_live,
    start_latents,
    latent_cotangent,
    media_gain,
    media_bias,
    latent_gain,
    latent_bias,
    w_query,
    w_kv,
    w_out,
    ff_gain,
    ff_bias,
    w_up,
    w_down,
):
    images, patches, width = media.shape
    latents = start_latents.shape[0]
    peers = lax.axis_size("dp")
    rows = images * latents
    fused = peers == 16
    wkv = w_kv[0]
    k = layers(
        fused,
        start_latents,
        media,
        latent_cotangent.reshape(rows, width),
        image_live,
        (media_gain, media_bias, latent_gain, latent_bias, ff_gain, ff_bias),
        w_query[0],
        wkv,
        w_out[0],
        w_up[0],
        w_down[0],
    )
    if fused:
        media_grad, start_grad, *rest = hand_over(
            latents,
            k.mine_out,
            k.theirs_out,
            k.small_out,
            k.start_out,
            [k.y_out, k.query_out, k.keyval_out, k.out_out, k.up_out, k.down_out],
        )
        lines = rest[:6]
        y_low, query, kv, out, up, down = rest[6:]
    else:
        mine, other, media_sums = media_grads(k.kv_out, media, wkv, media_gain)
        theirs = swap_sections(other)
        up, down, kv, query, out = (
            lax.psum_scatter(a, "dp", scatter_dimension=0, tiled=True).astype(F32)
            for a in (
                weight_grad(k.f_out, k.du_out.swapaxes(0, 1).reshape(rows, -1)),
                weight_grad(k.h_out.swapaxes(0, 1).reshape(rows, -1), k.g_out),
                weight_grad(k.j_out, k.kv_out),
                weight_grad(k.j_out[:, patches:], k.dq_out),
                weight_grad(k.o_out, k.dz1_out),
            )
        )
        y_low = k.y_out
        lines = jnp.concatenate([media_sums[:2], k.lines_out[2:6]], axis=0)
        lines = lax.psum_scatter(lines, "dp", scatter_dimension=1, tiled=True)
        lines = jnp.split(lines, 6, axis=0)
        start_part = lax.psum_scatter(
            k.lines_out[8 : 8 + latents], "dp", scatter_dimension=1, tiled=True
        )
        half = latents // 2
        far = swap_sections(start_part[half:])
        start_grad = jnp.where(lax.axis_index("section") == 0, start_part[:half], far)
        media_grad = mine + theirs.astype(F32)
    return (
        y_low.reshape(1, images, latents, width),
        media_grad,
        start_grad,
        *lines[:4],
        query[None],
        kv[None],
        out[None],
        *lines[4:],
        up[None],
        down[None],
    )


def solution(mesh):
    row = P("section", None)
    mat = P("section", None, None)
    in_specs = (
        P("dp", None, None), P("dp"), P(), P("dp", None, None),
        row, row, row, row, mat, mat, mat, row, row, mat, mat,
    )
    line = P("section", "dp")
    block = P("section", "dp", None)
    out_specs = (
        P("section", "dp", None, None), P("dp", None, "section"), line,
        line, line, line, line, block, block, block, line, line, block, block,
    )
    return jax.shard_map(shards, mesh=mesh, in_specs=in_specs, out_specs=out_specs, check_vma=False)
```
